256 devices in a mesh: seq: 16 (over z, x_hi), tp: 16 (over x_lo, y, core).
Axes of the slice: x: 4 (x_hi: 2, x_lo: 2; x = x_hi * 2 + x_lo), y: 4, z: 8, core: 2. Of those that a mesh axis runs over, the one named last changes fastest.
Arguments:
- hidden_in: bfloat16 [2048, 5120], P('seq'), may hold values from -64 to 64
- hidden_tan: bfloat16 [2048, 5120], P('seq'), may hold values from -6 to 6
- query_in: bfloat16 [2048, 4096], P('seq'), may hold values from -6 to 6
- key_in: bfloat16 [2048, 4096], P('seq'), may hold values from -6 to 6
- value_in: bfloat16 [2048, 4096], P('seq'), may hold values from -6 to 6
- query_tan: bfloat16 [2048, 4096], P('seq'), may hold values from -6 to 6
- key_tan: bfloat16 [2048, 4096], P('seq'), may hold values from -6 to 6
- value_tan: bfloat16 [2048, 4096], P('seq'), may hold values from -6 to 6
- output_weight: bfloat16 [4096, 5120], P(None, 'tp'), may hold values from -0.25 to 0.25
- feed_in: bfloat16 [5120, 6912], P('seq', 'tp'), may hold values from -0.078125 to 0.078125
- feed_out: bfloat16 [6912, 5120], P('tp', 'seq'), may hold values from -0.15625 to 0.15625
- modulation: float32 [4, 5120], replicated, may hold values from -4 to 4
- modulation_tan: float32 [4, 5120], replicated, may hold values from -4 to 4
- valid_rows: int32 [2048], replicated, may hold values 0 or 1
- first_frame: int32 [1], replicated, may hold values from 64 to 255
Outputs:
- block_out: bfloat16 [2048, 5120], P('seq', 'tp')
- block_tan: bfloat16 [2048, 5120], P('seq', 'tp')
The draws below stay inside these ranges and needn't reach their ends.
All inputs are finite; a program needn't handle non-finite values.
Results may differ from the reference program's by a relative error of at most 0.03.
Values may be sent and summed in bfloat16 or wider, within the bound.
A program may use at most 128 MiB of HBM per device.

```python
import jax
import jax.numpy as jnp
from jax import lax

D = 5120
HD = 128
FF = 6912
HEADS = 32
TOKENS = 2048


def draw_query_in(key, part):
    key = jax.random.fold_in(key, 1)
    values = jnp.clip(jax.random.normal(key, (TOKENS, HEADS * HD), jnp.float32) * 1.3, -6.0, 6.0)
    return values.astype(jnp.bfloat16)


def draw_key_in(key, part):
    key = jax.random.fold_in(key, 2)
    values = jnp.clip(jax.random.normal(key, (TOKENS, HEADS * HD), jnp.float32) * 1.3, -6.0, 6.0)
    return values.astype(jnp.bfloat16)


def draw_hidden_in(key, part):
    key = jax.random.fold_in(key, 3)
    row_scale = jnp.exp(jax.random.uniform(jax.random.fold_in(key, 1), (TOKENS, 1), jnp.float32, -1.15, 1.15))
    col_scale = jnp.exp(jax.random.uniform(jax.random.fold_in(key, 2), (1, D), jnp.float32, -1.15, 1.15))
    base = jnp.clip(jax.random.normal(jax.random.fold_in(key, 4), (TOKENS, D), jnp.float32), -6.0, 6.0)
    return (base * row_scale * col_scale).astype(jnp.bfloat16)


def touch_ends(drawn, stream_key, smallest, high):
    place = [jax.random.randint(jax.random.fold_in(stream_key, axis), (), 0, length) for axis, length in enumerate(drawn.shape)]
    widest = drawn.shape.index(max(drawn.shape))
    neighbour = place[:widest] + [(place[widest] + 1) % drawn.shape[widest]] + place[widest + 1:]
    return drawn.at[tuple(place)].set(smallest).at[tuple(neighbour)].set(high)


def block_levels(stream_key, shape, pieces, low, high):
    level, own = 1.0, jax.random.fold_in(stream_key, 6)
    for dim, shards_of in pieces:
        heights = jnp.exp(jax.random.uniform(jax.random.fold_in(own, dim), (shards_of,), jnp.float32, low / len(pieces), high / len(pieces)))
        level = level * jnp.repeat(heights, shape[dim] // shards_of).reshape([-1 if axis == dim else 1 for axis in range(len(shape))])
    return level


def scatter_about(key, extent, deviation, limit, pieces=(), kind=jnp.bfloat16):
    entries = deviation * jax.random.normal(key, extent, jnp.float32)
    if pieces:
        entries = entries * block_levels(key, extent, pieces, -0.22, 0.18)
    return jnp.clip(entries, -limit, limit).astype(kind)


def setup_inputs(seed: int = 0) -> dict:
    seeds = jax.random.split(jax.random.key(seed), 16)
    hidden_in = draw_hidden_in(jax.random.fold_in(seeds[15], 71), 0)
    hidden_tan = scatter_about(seeds[1], (TOKENS, D), 1.0, 6.0, ((0, 16),))
    query_in = draw_query_in(jax.random.fold_in(seeds[15], 71), 0)
    key_in = draw_key_in(jax.random.fold_in(seeds[15], 71), 0)
    value_in = scatter_about(seeds[4], (TOKENS, HEADS * HD), 1.0, 6.0, ((0, 16),))
    query_tan = scatter_about(seeds[5], (TOKENS, HEADS * HD), 1.0, 6.0, ((0, 16),))
    key_tan = scatter_about(seeds[6], (TOKENS, HEADS * HD), 1.0, 6.0, ((0, 16),))
    value_tan = scatter_about(seeds[7], (TOKENS, HEADS * HD), 1.0, 6.0, ((0, 16),))
    output_weight = scatter_about(seeds[8], (HEADS * HD, D), (HEADS * HD // 8) ** -0.5, 0.25, ((1, 16),))
    feed_in = scatter_about(seeds[9], (D, FF), D ** -0.5, 0.078125, ((0, 16), (1, 16)))
    feed_out = scatter_about(seeds[10], (FF, D), (FF // 4) ** -0.5, 0.15625, ((0, 16), (1, 16)))
    modulation = scatter_about(seeds[11], (4, D), 1.0, 4.0, (), jnp.float32)
    modulation_tan = scatter_about(seeds[12], (4, D), 1.0, 4.0, (), jnp.float32)
    valid_rows = touch_ends((jax.random.randint(seeds[13], (TOKENS,), 0, 8) < 7).astype(jnp.int32), jax.random.fold_in(seeds[13], 1), 0, 1)
    first_frame = jax.random.randint(seeds[14], (1,), TOKENS // 32, TOKENS // 8).astype(jnp.int32)
    return {"hidden_in": hidden_in, "hidden_tan": hidden_tan, "query_in": query_in, "key_in": key_in, "value_in": value_in, "query_tan": query_tan, "key_tan": key_tan, "value_tan": value_tan, "output_weight": output_weight, "feed_in": feed_in, "feed_out": feed_out, "modulation": modulation, "modulation_tan": modulation_tan, "valid_rows": valid_rows, "first_frame": first_frame}


def normalize(rows_in):
    centered = rows_in - lax.optimization_barrier(jnp.mean(rows_in, axis=-1, keepdims=True))
    spread = lax.optimization_barrier(jnp.mean(centered * centered, axis=-1, keepdims=True))
    return centered * lax.rsqrt(spread + 1e-06)

def gelu_tanh(values):
    return jax.nn.gelu(values, approximate=True)

def attend_head(inputs):
    query, keyed, valued, query_d, keyed_d, valued_d, valid = inputs
    factor = HD ** (-0.5)
    query = query.astype(jnp.float32)
    keyed = keyed.astype(jnp.float32)
    valued = valued.astype(jnp.float32)
    query_d = query_d.astype(jnp.float32)
    keyed_d = keyed_d.astype(jnp.float32)
    valued_d = valued_d.astype(jnp.float32)
    scores = jnp.dot(query, keyed.T) * factor
    scores_d = (jnp.dot(query_d, keyed.T) + jnp.dot(query, keyed_d.T)) * factor
    allowed = valid[None, :] > 0
    scores = jnp.where(allowed, scores, -1e+30)
    scores_d = jnp.where(allowed, scores_d, 0.0)
    top = lax.optimization_barrier(jnp.max(scores, axis=-1, keepdims=True))
    expo = jnp.exp(scores - top)
    probs = expo / lax.optimization_barrier(jnp.sum(expo, axis=-1, keepdims=True))
    probs_d = probs * (scores_d - lax.optimization_barrier(jnp.sum(probs * scores_d, axis=-1, keepdims=True)))
    probs_b = probs.astype(jnp.bfloat16).astype(jnp.float32)
    probs_db = probs_d.astype(jnp.bfloat16).astype(jnp.float32)
    attn = jnp.dot(probs_b, valued)
    attn_d = jnp.dot(probs_db, valued) + jnp.dot(probs_b, valued_d)
    return (attn.astype(jnp.bfloat16), attn_d.astype(jnp.bfloat16))

def reference(hidden_in, hidden_tan, query_in, key_in, value_in, query_tan, key_tan, value_tan, output_weight, feed_in, feed_out, modulation, modulation_tan, valid_rows, first_frame):
    positions = jnp.arange(TOKENS, dtype=jnp.int32)
    keep = (positions >= first_frame[0])[:, None]
    hidden_d = jnp.where(keep, hidden_tan, jnp.zeros_like(hidden_tan))
    query_d = jnp.where(keep, query_tan, jnp.zeros_like(query_tan))
    keyed_d = jnp.where(keep, key_tan, jnp.zeros_like(key_tan))
    valued_d = jnp.where(keep, value_tan, jnp.zeros_like(value_tan))

    def split(array):
        return array.reshape(TOKENS, HEADS, HD).transpose(1, 0, 2)

    def one_head(inputs):
        return attend_head(tuple(inputs) + (valid_rows,))
    attn, attn_d = lax.map(one_head, (split(query_in), split(key_in), split(value_in), split(query_d), split(keyed_d), split(valued_d)))
    attn = attn.transpose(1, 0, 2).reshape(TOKENS, HEADS * HD)
    attn_d = attn_d.transpose(1, 0, 2).reshape(TOKENS, HEADS * HD)
    proj = jnp.dot(attn, output_weight, preferred_element_type=jnp.float32).astype(jnp.bfloat16).astype(jnp.float32)
    proj_d = jnp.dot(attn_d, output_weight, preferred_element_type=jnp.float32).astype(jnp.bfloat16).astype(jnp.float32)
    gate_a, shift, scale, gate_f = (modulation[0], modulation[1], modulation[2], modulation[3])
    gate_ad, shift_d, scale_d, gate_fd = (modulation_tan[0], modulation_tan[1], modulation_tan[2], modulation_tan[3])
    resid = hidden_in.astype(jnp.float32) + gate_a * proj
    resid_d = hidden_d.astype(jnp.float32) + gate_ad * proj + gate_a * proj_d
    normed, normed_d = jax.jvp(normalize, (resid,), (resid_d,))
    shaped = (normed * (1.0 + scale) + shift).astype(jnp.bfloat16)
    shaped_d = (normed_d * (1.0 + scale) + normed * scale_d + shift_d).astype(jnp.bfloat16)
    pre = jnp.dot(shaped, feed_in, preferred_element_type=jnp.float32)
    pre_d = jnp.dot(shaped_d, feed_in, preferred_element_type=jnp.float32)
    act, act_d = jax.jvp(gelu_tanh, (pre,), (pre_d,))
    ffn = jnp.dot(act.astype(jnp.bfloat16), feed_out, preferred_element_type=jnp.float32)
    ffn_d = jnp.dot(act_d.astype(jnp.bfloat16), feed_out, preferred_element_type=jnp.float32)
    block_out = (resid + gate_f * ffn).astype(jnp.bfloat16)
    block_tan = (resid_d + gate_fd * ffn + gate_f * ffn_d).astype(jnp.bfloat16)
    return (block_out, block_tan)
```

```python
import jax
import jax.numpy as jnp
from jax import lax
from jax.experimental import pallas as pl
from jax.experimental.pallas import tpu as pltpu
from jax.sharding import PartitionSpec as P

D = 5120
HD = 128
WIDE = 320
HID = 432
ROWS = 128
SUB = 16
F32 = jnp.float32
BF16 = jnp.bfloat16
MESH = pl.DeviceIdType.MESH


def rem(a, b):
    return lax.rem(a, jnp.int32(b))


def div(a, b):
    return lax.div(a, jnp.int32(b))


def remote(src, dst, send, recv, device):
    return pltpu.make_async_remote_copy(
        src_ref=src, dst_ref=dst, send_sem=send, recv_sem=recv, device_id=device, device_id_type=MESH
    )


def dot_rows(a, b):
    return lax.dot_general(a, b, (((1,), (1,)), ((), ())), preferred_element_type=F32)


def kernel(
    first_ref, valid_ref, mod_ref, modt_ref,
    hid, hidt, q_in, k_in, v_in, q_tan, k_tan, v_tan, wo, w1, w2,
    out_ref, outt_ref,
    x6, grp, sc, dsc, pb, dpb, ao, at, hs, wob, wg1, wg2, ys, st, hb, pre, prex, act, ps, rb,
    lsem, wown, wosend, a1s, a1r, kvs, kvr, wr, ws, b1s, b1r, b2s, b2r, sts, str_, ds, dr, px, es, er,
):
    s = lax.axis_index("seq")
    t = lax.axis_index("tp")
    z, xh = div(s, 2), rem(s, 2)
    xl, y, c = div(t, 8), rem(div(t, 2), 4), rem(t, 2)
    x = 2 * xh + xl
    hf = rem(xl + xh, 2)
    yc = rem(t, 8)
    j = div(t, 2)
    plane = x * 4 + y
    sib = (s, t + 1 - 2 * c)

    def group(i):
        return (i, (rem(hf + rem(i, 2), 2) * 4 + y) * 2 + c)

    def plane_at(k):
        px_, py_ = rem(x + div(k, 4), 4), rem(y + rem(k, 4), 4)
        return px_, py_, (2 * z + div(px_, 2), (rem(px_, 2) * 4 + py_) * 2 + c)

    partner = (2 * z + c, (xl * 4 + y) * 2 + xh)
    up, down = (rem(s + 2, 16), t), (rem(s + 14, 16), t)

    my_rows = pl.ds(pl.multiple_of(yc * SUB, SUB), SUB)
    for n, ref in enumerate((q_in, q_tan, k_in, k_tan, v_in, v_tan)):
        pltpu.make_async_copy(ref.at[my_rows, :], x6.at[n], lsem.at[n]).start()
    start = pl.multiple_of(640 * j + 256 * c, 128)
    window = pl.ds(start, 384)
    load_h = pltpu.make_async_copy(hid.at[:, window], hs.at[0], lsem.at[6])
    load_ht = pltpu.make_async_copy(hidt.at[:, window], hs.at[1], lsem.at[7])
    load_wo = pltpu.make_async_copy(wo, wob, lsem.at[8])
    load_h.start()
    load_ht.start()
    load_wo.start()

    bar = pltpu.get_barrier_semaphore()

    def greet(k, _):
        pl.semaphore_signal(bar, inc=1, device_id=group(rem(s + k, 16)), device_id_type=MESH)
        pl.semaphore_signal(bar, inc=1, device_id=(s, rem(t + k, 16)), device_id_type=MESH)
        pl.semaphore_signal(bar, inc=1, device_id=plane_at(k)[2], device_id_type=MESH)
        return 0

    lax.fori_loop(1, 16, greet, 0)

    @pl.when(xh != c)
    def _():
        pl.semaphore_signal(bar, inc=1, device_id=partner, device_id_type=MESH)

    pl.semaphore_wait(bar, 45 + rem(xh + c, 2))

    for n, ref in enumerate((q_in, q_tan, k_in, k_tan, v_in, v_tan)):
        pltpu.make_async_copy(ref.at[my_rows, :], x6.at[n], lsem.at[n]).wait()
    first = first_ref[0]
    place = s * ROWS + yc * SUB + lax.broadcasted_iota(jnp.int32, (SUB, 1), 0)
    keep_sub = place >= first
    for n in (1, 3, 5):
        x6[n] = jnp.where(keep_sub, x6[n].astype(F32), 0.0).astype(BF16)

    def head_cols(i):
        head = div(i, 2) * 4 + 2 * hf + rem(i, 2)
        return pl.ds(pl.multiple_of(head * HD, HD), HD)

    def sub_of(i):
        return pl.ds(pl.multiple_of(yc * 256 + i * SUB, SUB), SUB)

    def a1(k):
        i = rem(s + k, 16)
        return remote(x6.at[:, :, head_cols(i)], grp.at[:, sub_of(s), :], a1s.at[k], a1r.at[s], group(i))

    a1_own = pltpu.make_async_copy(x6.at[:, :, head_cols(s)], grp.at[:, sub_of(s), :], a1r.at[s])
    a1_own.start()

    def a1_send(k, _):
        a1(k).start()
        return 0

    lax.fori_loop(1, 16, a1_send, 0)

    @pl.when(xh != c)
    def _():
        remote(w1, wg1.at[z], wosend.at[0], wown.at[0], partner).start()
        remote(w2, wg2.at[z], wosend.at[1], wown.at[1], partner).start()

    @pl.when(xh == c)
    def _():
        pltpu.make_async_copy(w1, wg1.at[z], wown.at[0]).start()
        pltpu.make_async_copy(w2, wg2.at[z], wown.at[1]).start()

    a1_own.wait()

    def a1_wait(k, _):
        i = rem(s + k, 16)
        remote(x6.at[:, :, head_cols(i)], grp.at[:, sub_of(i), :], a1s.at[k], a1r.at[i], group(i)).wait_recv()
        return 0

    lax.fori_loop(1, 16, a1_wait, 0)

    def slot_rows(slot):
        return pl.ds(pl.multiple_of(slot * 256, 256), 256)

    def kv(slot, n, device):
        view = grp.at[pl.ds(2, 4), slot_rows(slot), :]
        return remote(view, view, kvs.at[n], kvr.at[slot], device)

    def y_peer(k):
        yy = rem(y + k, 4)
        return yy * 2 + c, yy * 2 + 1 - c, (s, (xl * 4 + yy) * 2 + c)

    def kv_send(k, _):
        kv(yc, k, y_peer(k)[2]).start()
        return 0

    lax.fori_loop(1, 4, kv_send, 0)
    kv(yc, 4, sib).start()

    def ring(wg, slot, step, way, which):
        return remote(
            wg.at[slot], wg.at[slot], ws.at[step, way, which], wr.at[slot, which], (up, down)[way]
        )

    def ring_wait(slot, which):
        wg = (wg1, wg2)[which]
        ring(wg, slot, 0, 0, which).wait_recv()

    pltpu.make_async_copy(w1, wg1.at[z], wown.at[0]).wait()
    pltpu.make_async_copy(w2, wg2.at[z], wown.at[1]).wait()
    ring_sends = []

    def relay(step):
        below, above = rem(z + 8 - step, 8), rem(z + step, 8)
        if step > 0:
            for which in (0, 1):
                ring_wait(below, which)
                ring_wait(above, which)
        new = []
        if step < 3:
            for which in (0, 1):
                wg = (wg1, wg2)[which]
                new.append(ring(wg, below, step, 0, which))
                new.append(ring(wg, above, step, 1, which))
        else:
            new.append(ring(wg1, below, step, 0, 0))
            new.append(ring(wg2, above, step, 1, 1))
        for copy in new:
            copy.start()
        ring_sends.extend(new)

    relay(0)

    factor = HD ** (-0.5)
    own = slot_rows(yc)

    def score(slot):
        rows = slot_rows(slot)
        query = grp[0, own, :]
        keyed = grp[2, rows, :]
        both_q = jnp.concatenate([grp[1, own, :], query], axis=1)
        both_k = jnp.concatenate([keyed, grp[3, rows, :]], axis=1)
        allowed = valid_ref[:, rows] > 0
        sc[:, rows] = jnp.where(allowed, dot_rows(query, keyed) * factor, -1e30)
        dsc[:, rows] = jnp.where(allowed, dot_rows(both_q, both_k) * factor, 0.0)

    score(yc)
    kv(y * 2 + 1 - c, 0, sib).wait_recv()
    score(y * 2 + 1 - c)

    def score_peer(n, _):
        k = n + div(n, 2) - 2 * div(n, 3)
        same, other, device = y_peer(k)
        kv(same, k, device).wait_recv()
        kv(same, 4 + k, sib).start()
        score(same)
        kv(other, 0, sib).wait_recv()
        score(other)
        return 0

    lax.fori_loop(1, 4, score_peer, 0)

    def soft(n, _):
        rows = pl.ds(pl.multiple_of(n * SUB, SUB), SUB)
        values = sc[rows, :]
        expo = jnp.exp(values - jnp.max(values, axis=-1, keepdims=True))
        probs = expo * (1.0 / jnp.sum(expo, axis=-1, keepdims=True))
        tangent = dsc[rows, :]
        mean = jnp.sum(probs * tangent, axis=-1, keepdims=True)
        pb[rows, :] = probs.astype(BF16)
        dpb[rows, :] = (probs * (tangent - mean)).astype(BF16)
        return 0

    lax.fori_loop(0, 16, soft, 0)

    def weigh(n, _):
        rows = pl.ds(pl.multiple_of(n * 128, 128), 128)
        probs, tangent = pb[rows, :], dpb[rows, :]
        valued = grp[4]
        ao[0, rows, :] = jnp.dot(probs, valued, preferred_element_type=F32).astype(BF16)
        ao[1, rows, :] = (
            jnp.dot(tangent, valued, preferred_element_type=F32)
            + jnp.dot(probs, grp[5], preferred_element_type=F32)
        ).astype(BF16)
        return 0

    lax.fori_loop(0, 2, weigh, 0)

    def seq_cols(i):
        return pl.ds(pl.multiple_of(i * HD, HD), HD)

    def ao_rows(i):
        return pl.ds(pl.multiple_of(i * SUB, SUB), SUB)

    def b1(k):
        i = rem(s + k, 16)
        return remote(
            ao.at[:, ao_rows(i), :], at.at[hf, :, my_rows, seq_cols(s)], b1s.at[k], b1r.at[s], group(i)
        )

    b1_own = pltpu.make_async_copy(ao.at[:, ao_rows(s), :], at.at[hf, :, my_rows, seq_cols(s)], b1r.at[s])
    b1_own.start()

    def b1_send(k, _):
        b1(k).start()
        return 0

    lax.fori_loop(1, 16, b1_send, 0)
    relay(1)
    b1_own.wait()

    def b1_wait(k, _):
        i = rem(s + k, 16)
        remote(
            ao.at[:, ao_rows(i), :], at.at[hf, :, my_rows, seq_cols(i)], b1s.at[k], b1r.at[i], group(i)
        ).wait_recv()
        return 0

    lax.fori_loop(1, 16, b1_wait, 0)

    def piece(tt, n, device):
        xx, cc = div(tt, 8), rem(tt, 8)
        view = at.at[rem(xx + xh, 2), :, pl.ds(pl.multiple_of(cc * SUB, SUB), SUB), :]
        return remote(view, view, b2s.at[n], b2r.at[tt], device)

    def tp_peer(k):
        xx, yy = rem(xl + div(k, 4), 2), rem(y + rem(k, 4), 4)
        return (xx * 4 + yy) * 2 + c, (xx * 4 + yy) * 2 + 1 - c

    def b2_send(k, _):
        piece(t, k, (s, tp_peer(k)[0])).start()
        return 0

    lax.fori_loop(1, 8, b2_send, 0)
    piece(t, 8, sib).start()

    def b2_pass(k, _):
        same, _other = tp_peer(k)
        piece(same, k, (s, same)).wait_recv()
        piece(same, 8 + k, sib).start()
        return 0

    lax.fori_loop(1, 8, b2_pass, 0)

    def b2_wait(k, _):
        piece(tp_peer(k)[1], 8, sib).wait_recv()
        return 0

    lax.fori_loop(0, 8, b2_wait, 0)

    load_wo.wait()
    pre[:, 0:WIDE] = jnp.zeros((4 * ROWS, WIDE), F32)

    def project(n, _):
        cols = pl.ds(pl.multiple_of(n * 256, 256), 256)
        total = pre[0:256, 0:WIDE]
        for half in (0, 1):
            wrows = pl.ds(pl.multiple_of((4 * n + 2 * half) * HD, 256), 256)
            total += jnp.dot(
                at[half, :, :, cols].reshape(256, 256), wob[wrows, :], preferred_element_type=F32
            )
        pre[0:256, 0:WIDE] = total
        return 0

    lax.fori_loop(0, 8, project, 0)
    relay(2)

    def narrow(wide):
        return jnp.where(c == 0, wide[:, 0:WIDE], wide[:, 64 : 64 + WIDE])

    mod = narrow(mod_ref[:, window])
    modt = narrow(modt_ref[:, window])
    load_h.wait()
    load_ht.wait()
    keep = s * ROWS + lax.broadcasted_iota(jnp.int32, (ROWS, 1), 0) >= first
    proj = pre[0:ROWS, 0:WIDE].astype(BF16).astype(F32)
    proj_d = pre[ROWS : 2 * ROWS, 0:WIDE].astype(BF16).astype(F32)
    resid = narrow(hs[0].astype(F32)) + mod[0:1] * proj
    hid_d = jnp.where(keep, narrow(hs[1].astype(F32)), 0.0)
    resid_d = hid_d + modt[0:1] * proj + mod[0:1] * proj_d
    ys[0] = resid
    ys[1] = resid_d
    mean_i = jnp.mean(resid, axis=-1, keepdims=True)
    dmean_i = jnp.mean(resid_d, axis=-1, keepdims=True)
    cen = resid - mean_i
    square = jnp.sum(cen * cen, axis=-1, keepdims=True)
    cross = jnp.sum(cen * (resid_d - dmean_i), axis=-1, keepdims=True)
    lane = lax.broadcasted_iota(jnp.int32, (ROWS, ROWS), 1)
    packed = jnp.where(
        lane == 0, mean_i, jnp.where(lane == 1, dmean_i, jnp.where(lane == 2, square, cross))
    )
    st[t] = packed.T[0:8, :]

    def stat(k):
        return remote(st.at[t], st.at[t], sts.at[k], str_.at[t], (s, rem(t + k, 16)))

    def stat_send(k, _):
        stat(k).start()
        return 0

    lax.fori_loop(1, 16, stat_send, 0)

    def stat_wait(k, _):
        tt = rem(t + k, 16)
        remote(st.at[tt], st.at[tt], sts.at[k], str_.at[tt], (s, tt)).wait_recv()
        return 0

    lax.fori_loop(1, 16, stat_wait, 0)
    means, dmeans = st[:, 0, :], st[:, 1, :]
    mean_row = jnp.mean(means, axis=0, keepdims=True)
    dmean_row = jnp.mean(dmeans, axis=0, keepdims=True)
    off = means - mean_row
    var_row = (jnp.sum(st[:, 2, :], axis=0, keepdims=True) + WIDE * jnp.sum(off * off, axis=0, keepdims=True)) / D
    cov_row = (
        jnp.sum(st[:, 3, :], axis=0, keepdims=True)
        + WIDE * jnp.sum(off * (dmeans - dmean_row), axis=0, keepdims=True)
    ) / D
    inv_row = lax.rsqrt(var_row + 1e-06)
    bend_row = inv_row * inv_row * inv_row * cov_row
    line = lax.broadcasted_iota(jnp.int32, (ROWS, ROWS), 0)
    cols = jnp.where(
        line == 0, mean_row, jnp.where(line == 1, dmean_row, jnp.where(line == 2, inv_row, bend_row))
    ).T
    cen = resid - cols[:, 0:1]
    inv = cols[:, 2:3]
    normed = cen * inv
    normed_d = (resid_d - cols[:, 1:2]) * inv - cen * cols[:, 3:4]
    grow = 1.0 + mod[2:3]
    hb[j, xh, 0] = (normed * grow + mod[1:2]).astype(BF16)
    hb[j, xh, 1] = (normed_d * grow + normed * modt[2:3] + modt[1:2]).astype(BF16)

    def block(k):
        return remote(hb.at[j, xh], hb.at[j, xh], ds.at[k], dr.at[plane], plane_at(k)[2])

    def block_send(k, _):
        block(k).start()
        return 0

    lax.fori_loop(1, 16, block_send, 0)
    relay(3)

    def block_wait(jj, ee):
        view = hb.at[jj, ee]
        source = (2 * ee + div(jj, 4)) * 4 + rem(jj, 4)
        remote(view, view, ds.at[0], dr.at[source], sib).wait_recv()

    def feed_at(k):
        return rem(xl + div(k, 4), 2) * 4 + rem(y + rem(k, 4), 4)

    def feed(jj):
        return jnp.dot(hb[jj].reshape(4 * ROWS, WIDE), wg1[jj], preferred_element_type=F32)

    far = rem(z + 4, 8)
    ring_wait(far, 0)
    block_wait(j, 1 - xh)
    pre[...] = feed(j)

    def feed_step(k, _):
        jj = feed_at(k)
        block_wait(jj, xh)
        block_wait(jj, 1 - xh)
        pre[...] += feed(jj)
        return 0

    lax.fori_loop(1, 8, feed_step, 0)

    mine = pl.ds(pl.multiple_of(c * 256, 256), 256)
    others = pl.ds(pl.multiple_of((1 - c) * 256, 256), 256)
    swap = remote(pre.at[others, :], prex, px.at[0], px.at[1], sib)
    swap.start()
    swap.wait_recv()
    total = pre[mine, :] + prex[...]
    before, before_d = total[0:ROWS], total[ROWS : 2 * ROWS]
    root = 0.7978845608028654
    cube = 0.044715
    squared = before * before
    bent = jnp.tanh(root * (before + cube * squared * before))
    half = 0.5 * (1.0 + bent)
    slope = half + 0.5 * before * (1.0 - bent * bent) * (root * (1.0 + 3.0 * cube * squared))
    act[mine, :] = jnp.concatenate([before * half, slope * before_d], axis=0).astype(BF16)
    share = remote(act.at[mine, :], act.at[mine, :], px.at[2], px.at[3], sib)
    share.start()
    ring_wait(far, 1)
    remote(act.at[others, :], act.at[others, :], px.at[2], px.at[3], sib).wait_recv()

    def terms(jj):
        ps[jj] = (
            jnp.dot(act[...], wg2[jj], preferred_element_type=F32).astype(BF16).reshape(2, 2, ROWS, WIDE)
        )

    def part(jj, ee, n):
        device = (2 * z + ee, jj * 2 + c)
        return remote(ps.at[jj, ee], rb.at[plane], es.at[n], er.at[plane], device)

    def term_step(k, _):
        jj = feed_at(k)
        terms(jj)
        part(jj, xh, 2 * k).start()
        part(jj, 1 - xh, 2 * k + 1).start()
        return 0

    lax.fori_loop(1, 8, term_step, 0)
    terms(j)
    part(j, 1 - xh, 1).start()
    ys_own = ps[j, xh].astype(F32)
    rb_sum = [ys_own[0], ys_own[1]]

    def sum_step(k, carry):
        px_, py_, _device = plane_at(k)
        source = px_ * 4 + py_
        remote(ps.at[0, 0], rb.at[source], es.at[0], er.at[source], sib).wait_recv()
        return carry[0] + rb[source, 0].astype(F32), carry[1] + rb[source, 1].astype(F32)

    ffn, ffn_d = lax.fori_loop(1, 16, sum_step, tuple(rb_sum))
    out_ref[...] = (ys[0] + mod[3:4] * ffn).astype(BF16)
    outt_ref[...] = (ys[1] + modt[3:4] * ffn + mod[3:4] * ffn_d).astype(BF16)

    def drain16(k, _):
        a1(k).wait_send()
        b1(k).wait_send()
        stat(k).wait_send()
        block(k).wait_send()
        return 0

    lax.fori_loop(1, 16, drain16, 0)

    def drain_kv(k, _):
        kv(yc, k, sib).wait_send()
        return 0

    lax.fori_loop(1, 8, drain_kv, 0)

    def drain_b2(k, _):
        piece(t, k, sib).wait_send()
        return 0

    lax.fori_loop(1, 16, drain_b2, 0)

    def drain_part(k, _):
        part(j, 1 - xh, k).wait_send()
        return 0

    lax.fori_loop(1, 16, drain_part, 0)
    for copy in ring_sends:
        copy.wait_send()
    swap.wait_send()
    share.wait_send()

    @pl.when(xh != c)
    def _():
        remote(w1, wg1.at[z], wosend.at[0], wown.at[0], partner).wait_send()
        remote(w2, wg2.at[z], wosend.at[1], wown.at[1], partner).wait_send()


def local(
    hidden_in, hidden_tan, query_in, key_in, value_in, query_tan, key_tan, value_tan,
    output_weight, feed_in, feed_out, modulation, modulation_tan, valid_rows, first_frame,
):
    valid = valid_rows.reshape(16, 8, SUB).transpose(1, 0, 2).reshape(1, 2048)
    vmem = pl.BlockSpec(memory_space=pltpu.VMEM)
    hbm = pl.BlockSpec(memory_space=pl.ANY)
    dma = pltpu.SemaphoreType.DMA
    shape = jax.ShapeDtypeStruct((ROWS, WIDE), BF16)
    return pl.pallas_call(
        kernel,
        out_shape=(shape, shape),
        in_specs=[pl.BlockSpec(memory_space=pltpu.SMEM)] + [vmem] * 3 + [hbm] * 11,
        out_specs=(vmem, vmem),
        scratch_shapes=[
            pltpu.VMEM((6, SUB, 4096), BF16),
            pltpu.VMEM((6, 2048, HD), BF16),
            pltpu.VMEM((256, 2048), F32),
            pltpu.VMEM((256, 2048), F32),
            pltpu.VMEM((256, 2048), BF16),
            pltpu.VMEM((256, 2048), BF16),
            pltpu.VMEM((2, 256, HD), BF16),
            pltpu.VMEM((2, 2, ROWS, 2048), BF16),
            pltpu.VMEM((2, ROWS, 384), BF16),
            pltpu.VMEM((4096, WIDE), BF16),
            pltpu.VMEM((8, WIDE, HID), BF16),
            pltpu.VMEM((8, HID, WIDE), BF16),
            pltpu.VMEM((2, ROWS, WIDE), F32),
            pltpu.VMEM((16, 8, ROWS), F32),
            pltpu.VMEM((8, 2, 2, ROWS, WIDE), BF16),
            pltpu.VMEM((4 * ROWS, HID), F32),
            pltpu.VMEM((2 * ROWS, HID), F32),
            pltpu.VMEM((4 * ROWS, HID), BF16),
            pltpu.VMEM((8, 2, 2, ROWS, WIDE), BF16),
            pltpu.VMEM((16, 2, ROWS, WIDE), BF16),
            dma((9,)),
            dma((2,)),
            dma((2,)),
            dma((16,)),
            dma((16,)),
            dma((8,)),
            dma((8,)),
            dma((8, 2)),
            dma((4, 2, 2)),
            dma((16,)),
            dma((16,)),
            dma((16,)),
            dma((16,)),
            dma((16,)),
            dma((16,)),
            dma((16,)),
            dma((16,)),
            dma((4,)),
            dma((16,)),
            dma((16,)),
        ],
        compiler_params=pltpu.CompilerParams(
            collective_id=0, has_side_effects=True, vmem_limit_bytes=56 * 1024 * 1024
        ),
        cost_estimate=pl.CostEstimate(flops=4_000_000_000, bytes_accessed=20_000_000, transcendentals=1_000_000),
    )(
        first_frame, valid, modulation, modulation_tan,
        hidden_in, hidden_tan, query_in, key_in, value_in, query_tan, key_tan, value_tan,
        output_weight, feed_in, feed_out,
    )


def solution(mesh):
    rows = P("seq", None)
    placed = (rows,) * 8 + (P(None, "tp"), P("seq", "tp"), P("tp", "seq"), P(), P(), P(), P())
    return jax.shard_map(
        local, mesh=mesh, in_specs=placed, out_specs=(P("seq", "tp"), P("seq", "tp")), check_vma=False
    )
```

```python
import jax
import jax.numpy as jnp
from jax import lax
from jax.experimental import pallas as pl
from jax.experimental.pallas import tpu as pltpu
from jax.sharding import PartitionSpec as P

D = 5120
HD = 128
WIDE = 320
HID = 432
PACK = 896
ROWS = 128
SUB = 16
F32 = jnp.float32
BF16 = jnp.bfloat16
MESH = pl.DeviceIdType.MESH


def rem(a, b):
    return lax.rem(a, jnp.int32(b))


def div(a, b):
    return lax.div(a, jnp.int32(b))


def remote(src, dst, send, recv, device):
    return pltpu.make_async_remote_copy(
        src_ref=src, dst_ref=dst, send_sem=send, recv_sem=recv, device_id=device, device_id_type=MESH
    )


def dot_rows(a, b):
    return lax.dot_general(a, b, (((1,), (1,)), ((), ())), preferred_element_type=F32)


def kernel(
    first_ref, valid_ref, mod_ref, modt_ref,
    hid, hidt, q_in, k_in, v_in, q_tan, k_tan, v_tan, wo, w1, w2,
    out_ref, outt_ref,
    x6, grp, sc, dsc, pb, dpb, ao, at, hs, wob, wload, wown, wg, ys, st, hb, pre, prex, act,
    ps, ra, rb, ta, rc, rd,
    lsem, wsem, a1s, a1r, kvs, kvr, wr, ws, b1s, b1r, b2s, b2r, sts, str_, ds, dr, px, es, er,
):
    s = lax.axis_index("seq")
    t = lax.axis_index("tp")
    z, xh = div(s, 2), rem(s, 2)
    xl, y, c = div(t, 8), rem(div(t, 2), 4), rem(t, 2)
    x = 2 * xh + xl
    hf = rem(xl + xh, 2)
    yc = rem(t, 8)
    j = div(t, 2)
    plane = x * 4 + y
    sib = (s, t + 1 - 2 * c)

    def group(i):
        return (i, (rem(hf + rem(i, 2), 2) * 4 + y) * 2 + c)

    def chip(xx, yy):
        return (2 * z + div(xx, 2), (rem(xx, 2) * 4 + yy) * 2 + c)

    partner = (2 * z + c, ((1 - xl) * 4 + y) * 2 + xh)
    up, down = (rem(s + 2, 16), t), (rem(s + 14, 16), t)

    my_rows = pl.ds(pl.multiple_of(yc * SUB, SUB), SUB)
    streams = (q_in, q_tan, k_in, k_tan, v_in, v_tan)

    def load(n):
        return pltpu.make_async_copy(streams[n].at[my_rows, :], x6.at[n], lsem.at[n])

    for n in range(6):
        load(n).start()
    load_w1 = pltpu.make_async_copy(w1, wload.at[0], lsem.at[9])
    load_w2 = pltpu.make_async_copy(w2, wload.at[1], lsem.at[10])
    load_w1.start()
    load_w2.start()
    start = pl.multiple_of(640 * j + 256 * c, 128)
    window = pl.ds(start, 384)
    load_h = pltpu.make_async_copy(hid.at[:, window], hs.at[0], lsem.at[6])
    load_ht = pltpu.make_async_copy(hidt.at[:, window], hs.at[1], lsem.at[7])
    load_wo = pltpu.make_async_copy(wo, wob, lsem.at[8])
    load_h.start()
    load_ht.start()
    load_wo.start()

    bar = pltpu.get_barrier_semaphore()

    def greet(k, _):
        pl.semaphore_signal(bar, inc=1, device_id=group(rem(s + k, 16)), device_id_type=MESH)
        pl.semaphore_signal(bar, inc=1, device_id=(s, rem(t + k, 16)), device_id_type=MESH)
        return 0

    lax.fori_loop(1, 16, greet, 0)
    pl.semaphore_signal(bar, inc=1, device_id=partner, device_id_type=MESH)
    for n in range(6):
        load(n).wait()
    first = first_ref[0]
    place = s * ROWS + yc * SUB + lax.broadcasted_iota(jnp.int32, (SUB, 1), 0)
    keep_sub = place >= first
    for n in (1, 3, 5):
        x6[n] = jnp.where(keep_sub, x6[n].astype(F32), 0.0).astype(BF16)
    load_w1.wait()
    load_w2.wait()
    wown[:, 0:HID] = wload[0]
    wown[:, HID : 2 * HID] = wload[1]
    wown[:, 2 * HID :] = jnp.zeros((WIDE, PACK - 2 * HID), BF16)
    pl.semaphore_wait(bar, 31)

    def head_cols(i):
        head = div(i, 2) * 4 + 2 * hf + rem(i, 2)
        return pl.ds(pl.multiple_of(head * HD, HD), HD)

    def sub_of(i):
        return pl.ds(pl.multiple_of(yc * 256 + i * SUB, SUB), SUB)

    def a1(k):
        i = rem(s + k, 16)
        return remote(x6.at[:, :, head_cols(i)], grp.at[:, sub_of(s), :], a1s.at[k], a1r.at[s], group(i))

    a1_own = pltpu.make_async_copy(x6.at[:, :, head_cols(s)], grp.at[:, sub_of(s), :], a1r.at[s])
    a1_own.start()

    def a1_send(k, _):
        a1(k).start()
        return 0

    lax.fori_loop(1, 16, a1_send, 0)

    to_ring = remote(wown, wg.at[z], wsem.at[0], wsem.at[1], partner)
    to_ring.start()
    ring_sends = []

    def ring(slot, step, way):
        view = wg.at[slot]
        if step == 3:
            view = view.at[pl.ds((0, WIDE // 2)[way], WIDE // 2), :]
        return remote(view, view, ws.at[step, way], wr.at[slot], (up, down)[way])

    def ring_wait(slot):
        ring(slot, 0, 0).wait_recv()

    def relay(step):
        below, above = rem(z + 8 - step, 8), rem(z + step, 8)
        if step > 0:
            ring_wait(below)
            ring_wait(above)
        for copy in (ring(below, step, 0), ring(above, step, 1)):
            copy.start()
            ring_sends.append(copy)

    to_ring.wait_recv()
    relay(0)
    a1_own.wait()

    def a1_wait(k, _):
        i = rem(s + k, 16)
        remote(x6.at[:, :, head_cols(i)], grp.at[:, sub_of(i), :], a1s.at[k], a1r.at[i], group(i)).wait_recv()
        return 0

    lax.fori_loop(1, 16, a1_wait, 0)

    def slot_rows(slot):
        return pl.ds(pl.multiple_of(slot * 256, 256), 256)

    def kv(slot, n, device, low=2, count=4):
        view = grp.at[pl.ds(low, count), slot_rows(slot), :]
        return remote(view, view, kvs.at[n], kvr.at[slot], device)

    y_up, y_down, y_far = rem(y + 1, 4), rem(y + 3, 4), rem(y + 2, 4)
    x_up, x_down, x_far = rem(x + 1, 4), rem(x + 3, 4), rem(x + 2, 4)

    def column(yy):
        return (s, (xl * 4 + yy) * 2 + c)

    def same(yy):
        return yy * 2 + c

    def other(yy):
        return yy * 2 + 1 - c

    kv_sends = [
        kv(yc, 0, column(y_up)),
        kv(yc, 1, column(y_down)),
        kv(yc, 2, sib),
        kv(same(y_down), 3, column(y_up), 2, 2),
        kv(same(y_down), 4, sib),
        kv(same(y_up), 5, column(y_down), 4, 2),
        kv(same(y_up), 6, sib),
        kv(same(y_far), 7, sib),
    ]

    def kv_wait(slot):
        kv(slot, 0, sib).wait_recv()

    for copy in kv_sends[0:3]:
        copy.start()

    factor = HD ** (-0.5)
    own = slot_rows(yc)
    valid = valid_ref[...].astype(F32).astype(BF16)
    from_lane = lax.broadcasted_iota(jnp.int32, (ROWS, 256), 0)
    to_lane = lax.broadcasted_iota(jnp.int32, (ROWS, 256), 1)
    shard_line = lax.broadcasted_iota(jnp.int32, (16, 256), 0)
    shard_lane = div(lax.broadcasted_iota(jnp.int32, (16, 256), 1), SUB)

    def score(slot):
        rows = slot_rows(slot)
        pick = jnp.where(from_lane == slot * SUB + rem(to_lane, SUB), 1.0, 0.0).astype(BF16)
        spread = jnp.dot(valid, pick, preferred_element_type=F32)
        allowed = jnp.sum(jnp.where(shard_line == shard_lane, spread, 0.0), axis=0, keepdims=True) > 0.5
        query = grp[0, own, :]
        keyed = grp[2, rows, :]
        both_q = jnp.concatenate([grp[1, own, :], query], axis=1)
        both_k = jnp.concatenate([keyed, grp[3, rows, :]], axis=1)
        sc[:, rows] = jnp.where(allowed, dot_rows(query, keyed) * factor, -1e30)
        dsc[:, rows] = jnp.where(allowed, dot_rows(both_q, both_k) * factor, 0.0)

    score(yc)
    kv_wait(other(y))
    score(other(y))
    kv_wait(same(y_down))
    kv_sends[3].start()
    kv_sends[4].start()
    kv_wait(same(y_up))
    kv_sends[5].start()
    kv_sends[6].start()
    score(same(y_down))
    score(same(y_up))
    kv_wait(other(y_down))
    score(other(y_down))
    kv_wait(other(y_up))
    score(other(y_up))
    kv_wait(same(y_far))
    kv_sends[7].start()
    score(same(y_far))
    kv_wait(other(y_far))
    score(other(y_far))
    relay(1)

    def soft(n, _):
        rows = pl.ds(pl.multiple_of(n * SUB, SUB), SUB)
        values = sc[rows, :]
        expo = jnp.exp(values - jnp.max(values, axis=-1, keepdims=True))
        probs = expo * (1.0 / jnp.sum(expo, axis=-1, keepdims=True))
        tangent = dsc[rows, :]
        mean = jnp.sum(probs * tangent, axis=-1, keepdims=True)
        pb[rows, :] = probs.astype(BF16)
        dpb[rows, :] = (probs * (tangent - mean)).astype(BF16)
        return 0

    lax.fori_loop(0, 16, soft, 0)

    def weigh(n, _):
        rows = pl.ds(pl.multiple_of(n * 128, 128), 128)
        probs, tangent = pb[rows, :], dpb[rows, :]
        valued = grp[4]
        ao[0, rows, :] = jnp.dot(probs, valued, preferred_element_type=F32).astype(BF16)
        ao[1, rows, :] = (
            jnp.dot(tangent, valued, preferred_element_type=F32)
            + jnp.dot(probs, grp[5], preferred_element_type=F32)
        ).astype(BF16)
        return 0

    lax.fori_loop(0, 2, weigh, 0)

    def seq_cols(i):
        return pl.ds(pl.multiple_of(i * HD, HD), HD)

    def ao_rows(i):
        return pl.ds(pl.multiple_of(i * SUB, SUB), SUB)

    def b1(k):
        i = rem(s + k, 16)
        return remote(
            ao.at[:, ao_rows(i), :], at.at[hf, :, my_rows, seq_cols(s)], b1s.at[k], b1r.at[s], group(i)
        )

    b1_own = pltpu.make_async_copy(ao.at[:, ao_rows(s), :], at.at[hf, :, my_rows, seq_cols(s)], b1r.at[s])
    b1_own.start()

    def b1_send(k, _):
        b1(k).start()
        return 0

    lax.fori_loop(1, 16, b1_send, 0)
    b1_own.wait()

    def b1_wait(k, _):
        i = rem(s + k, 16)
        remote(
            ao.at[:, ao_rows(i), :], at.at[hf, :, my_rows, seq_cols(i)], b1s.at[k], b1r.at[i], group(i)
        ).wait_recv()
        return 0

    lax.fori_loop(1, 16, b1_wait, 0)

    def piece(xx, cc, n, device, low=0, count=2):
        rows = pl.ds(pl.multiple_of(cc * SUB, SUB), SUB)
        view = at.at[rem(xx + xh, 2), pl.ds(low, count), rows, :]
        return remote(view, view, b2s.at[n], b2r.at[xx * 8 + cc], device)

    def piece_wait(xx, cc):
        piece(xx, cc, 0, sib).wait_recv()

    across = (s, ((1 - xl) * 4 + y) * 2 + c)
    b2_sends = [
        piece(xl, yc, 0, across),
        piece(xl, yc, 1, column(y_up)),
        piece(xl, yc, 2, column(y_down)),
        piece(xl, yc, 3, sib),
        piece(1 - xl, yc, 4, column(y_up)),
        piece(1 - xl, yc, 5, column(y_down)),
        piece(1 - xl, yc, 6, sib),
    ]
    for n, xx in enumerate((xl, 1 - xl)):
        b2_sends += [
            piece(xx, same(y_down), 7 + 5 * n, column(y_up), 0, 1),
            piece(xx, same(y_down), 8 + 5 * n, sib),
            piece(xx, same(y_up), 9 + 5 * n, column(y_down), 1, 1),
            piece(xx, same(y_up), 10 + 5 * n, sib),
            piece(xx, same(y_far), 11 + 5 * n, sib),
        ]
    for copy in b2_sends[0:4]:
        copy.start()
    piece_wait(1 - xl, yc)
    for copy in b2_sends[4:7]:
        copy.start()
    relay(2)
    for n, xx in enumerate((xl, 1 - xl)):
        piece_wait(xx, same(y_down))
        b2_sends[7 + 5 * n].start()
        b2_sends[8 + 5 * n].start()
        piece_wait(xx, same(y_up))
        b2_sends[9 + 5 * n].start()
        b2_sends[10 + 5 * n].start()
    for n, xx in enumerate((xl, 1 - xl)):
        piece_wait(xx, same(y_far))
        b2_sends[11 + 5 * n].start()
    for xx in (xl, 1 - xl):
        for yy in (y, y_down, y_up, y_far):
            piece_wait(xx, other(yy))

    load_wo.wait()
    pre[:, 0:WIDE] = jnp.zeros((4 * ROWS, WIDE), F32)

    def project(n, _):
        cols = pl.ds(pl.multiple_of(n * 256, 256), 256)
        total = pre[0:256, 0:WIDE]
        for half in (0, 1):
            heads = pl.ds(pl.multiple_of((4 * n + 2 * half) * HD, 256), 256)
            total += dot_rows(at[half, :, :, cols].reshape(256, 256), wob[:, heads])
        pre[0:256, 0:WIDE] = total
        return 0

    lax.fori_loop(0, 8, project, 0)

    def narrow(wide):
        return jnp.where(c == 0, wide[:, 0:WIDE], wide[:, 64 : 64 + WIDE])

    mod = narrow(mod_ref[:, window])
    modt = narrow(modt_ref[:, window])
    load_h.wait()
    load_ht.wait()
    keep = s * ROWS + lax.broadcasted_iota(jnp.int32, (ROWS, 1), 0) >= first
    proj = pre[0:ROWS, 0:WIDE].astype(BF16).astype(F32)
    proj_d = pre[ROWS : 2 * ROWS, 0:WIDE].astype(BF16).astype(F32)
    resid = narrow(hs[0].astype(F32)) + mod[0:1] * proj
    hid_d = jnp.where(keep, narrow(hs[1].astype(F32)), 0.0)
    resid_d = hid_d + modt[0:1] * proj + mod[0:1] * proj_d
    ys[0] = resid
    ys[1] = resid_d
    mean_i = jnp.mean(resid, axis=-1, keepdims=True)
    dmean_i = jnp.mean(resid_d, axis=-1, keepdims=True)
    cen = resid - mean_i
    square = jnp.sum(cen * cen, axis=-1, keepdims=True)
    cross = jnp.sum(cen * (resid_d - dmean_i), axis=-1, keepdims=True)
    lane = lax.broadcasted_iota(jnp.int32, (ROWS, ROWS), 1)
    packed = jnp.where(
        lane == 0, mean_i, jnp.where(lane == 1, dmean_i, jnp.where(lane == 2, square, cross))
    )
    st[t] = packed.T[0:8, :]

    def stat(k):
        return remote(st.at[t], st.at[t], sts.at[k], str_.at[t], (s, rem(t + k, 16)))

    def stat_send(k, _):
        stat(k).start()
        return 0

    lax.fori_loop(1, 16, stat_send, 0)

    def stat_wait(k, _):
        tt = rem(t + k, 16)
        remote(st.at[tt], st.at[tt], sts.at[k], str_.at[tt], (s, tt)).wait_recv()
        return 0

    lax.fori_loop(1, 16, stat_wait, 0)
    means, dmeans = st[:, 0, :], st[:, 1, :]
    mean_row = jnp.mean(means, axis=0, keepdims=True)
    dmean_row = jnp.mean(dmeans, axis=0, keepdims=True)
    off = means - mean_row
    var_row = (jnp.sum(st[:, 2, :], axis=0, keepdims=True) + WIDE * jnp.sum(off * off, axis=0, keepdims=True)) / D
    cov_row = (
        jnp.sum(st[:, 3, :], axis=0, keepdims=True)
        + WIDE * jnp.sum(off * (dmeans - dmean_row), axis=0, keepdims=True)
    ) / D
    inv_row = lax.rsqrt(var_row + 1e-06)
    bend_row = inv_row * inv_row * inv_row * cov_row
    line = lax.broadcasted_iota(jnp.int32, (ROWS, ROWS), 0)
    cols = jnp.where(
        line == 0, mean_row, jnp.where(line == 1, dmean_row, jnp.where(line == 2, inv_row, bend_row))
    ).T
    cen = resid - cols[:, 0:1]
    inv = cols[:, 2:3]
    normed = cen * inv
    normed_d = (resid_d - cols[:, 1:2]) * inv - cen * cols[:, 3:4]
    grow = 1.0 + mod[2:3]
    hb[plane, :, 0:WIDE] = (normed * grow + mod[1:2]).astype(BF16)
    hb[plane, :, WIDE:] = (normed_d * grow + normed * modt[2:3] + modt[1:2]).astype(BF16)

    axes = (((x, x_up, x_down, x_far), (y, y_up, y_down, y_far)), ((y, y_up, y_down, y_far), (x, x_up, x_down, x_far)))
    SELF, UP, DOWN, FAR = range(4)

    def at_chip(flow, first_place, second_place):
        a, b = axes[flow][0][first_place], axes[flow][1][second_place]
        return (a, b) if flow == 0 else (b, a)

    block_sends = []

    def block(flow, first_place, second_place, low=0, count=64):
        xx, yy = at_chip(flow, first_place, second_place)
        slot = xx * 4 + yy
        view = hb.at[slot, pl.ds(64 * flow + low, count), :]
        return lambda n, device: remote(view, view, ds.at[flow, n], dr.at[flow, slot], device)

    counts = [0, 0]

    def block_send(flow, made, device):
        copy = made(counts[flow], device)
        counts[flow] += 1
        copy.start()
        block_sends.append(copy)

    def block_wait(flow, first_place, second_place):
        block(flow, first_place, second_place)(0, sib).wait_recv()

    def beside(flow, first_place, second_place):
        return chip(*at_chip(flow, first_place, second_place))

    def spread_second(flow, first_place):
        for way in (UP, DOWN):
            block_send(flow, block(flow, first_place, SELF), beside(flow, SELF, way))

    def pass_second(flow, first_place):
        block_wait(flow, first_place, DOWN)
        block_send(flow, block(flow, first_place, DOWN, 0, 32), beside(flow, SELF, UP))
        block_wait(flow, first_place, UP)
        block_send(flow, block(flow, first_place, UP, 32, 32), beside(flow, SELF, DOWN))

    for flow in (0, 1):
        for way in (UP, DOWN):
            block_send(flow, block(flow, SELF, SELF), beside(flow, way, SELF))
    for flow in (0, 1):
        spread_second(flow, SELF)
    for flow in (0, 1):
        block_wait(flow, DOWN, SELF)
        block_send(flow, block(flow, DOWN, SELF, 0, 32), beside(flow, UP, SELF))
        block_wait(flow, UP, SELF)
        block_send(flow, block(flow, UP, SELF, 32, 32), beside(flow, DOWN, SELF))
    for flow in (0, 1):
        spread_second(flow, DOWN)
        spread_second(flow, UP)
    for flow in (0, 1):
        block_wait(flow, FAR, SELF)
        spread_second(flow, FAR)
    relay(3)
    for first_place in (SELF, DOWN, UP, FAR):
        for flow in (0, 1):
            pass_second(flow, first_place)

    def feed(xx, yy):
        lower, upper = hb[xx * 4 + yy], hb[(xx + 2) * 4 + yy]
        rows = jnp.concatenate(
            [lower[:, 0:WIDE], lower[:, WIDE:], upper[:, 0:WIDE], upper[:, WIDE:]], axis=0
        )
        return jnp.dot(rows, wg[xx * 4 + yy, :, 0:HID], preferred_element_type=F32)

    ring_wait(rem(z + 4, 8))
    pre[...] = feed(1 - xl, y)
    pre[...] += feed(1 - xl, y_up)
    pre[...] += feed(1 - xl, y_down)
    for first_place in (SELF, DOWN, UP, FAR):
        for flow in (0, 1):
            block_wait(flow, first_place, FAR)
    pre[...] += feed(1 - xl, y_far)

    def feed_step(yy, _):
        pre[...] += feed(xl, yy)
        return 0

    lax.fori_loop(0, 4, feed_step, 0)

    mine = pl.ds(pl.multiple_of(c * 256, 256), 256)
    others = pl.ds(pl.multiple_of((1 - c) * 256, 256), 256)
    swap = remote(pre.at[others, :], prex, px.at[0], px.at[1], sib)
    swap.start()
    swap.wait_recv()
    total = pre[mine, :] + prex[...]
    before, before_d = total[0:ROWS], total[ROWS : 2 * ROWS]
    root = 0.7978845608028654
    cube = 0.044715
    squared = before * before
    bent = jnp.tanh(root * (before + cube * squared * before))
    half = 0.5 * (1.0 + bent)
    slope = half + 0.5 * before * (1.0 - bent * bent) * (root * (1.0 + 3.0 * cube * squared))
    stacked = jnp.concatenate([before * half, slope * before_d], axis=0).astype(BF16)
    act[mine, :] = jnp.concatenate(
        [jnp.zeros((256, 48), BF16), stacked, jnp.zeros((256, 32), BF16)], axis=1
    )
    share = remote(act.at[mine, :], act.at[mine, :], px.at[2], px.at[3], sib)
    share.start()
    remote(act.at[others, :], act.at[others, :], px.at[2], px.at[3], sib).wait_recv()

    def terms(xx, yy):
        parts = dot_rows(act[...], wg[xx * 4 + yy, :, PACK - 512 :]).astype(BF16)
        for ee in (0, 1):
            both = jnp.concatenate([parts[256 * ee : 256 * ee + 128], parts[256 * ee + 128 : 256 * ee + 256]], axis=1)
            ps[0, yy, xx + 2 * ee] = both[0:64]
            ps[1, xx + 2 * ee, yy] = both[64:128]

    major = ((y, y_up, y_down, y_far), (x, x_up, x_down, x_far))
    toward = (
        ((chip(x, y_up), chip(x, y_down)), (chip(x_up, y), chip(x_down, y))),
        ((chip(x_up, y), chip(x_down, y)), (chip(x, y_up), chip(x, y_down))),
    )
    sum_sends = []

    def sum_send(flow, n, src, dst, phase, way):
        copy = remote(src, dst, es.at[flow, n], er.at[flow, n], toward[flow][phase][way])
        copy.start()
        sum_sends.append(copy)

    def sum_wait(flow, n, dst):
        remote(dst, dst, es.at[flow, n], er.at[flow, n], sib).wait_recv()

    def far_out(flow):
        for way in (0, 1):
            src = ps.at[flow, major[flow][FAR], :, pl.ds(32 * way, 32), :]
            sum_send(flow, way, src, ra.at[flow, way], 0, way)

    def near_out(flow):
        for way in (0, 1):
            sum_wait(flow, way, ra.at[flow, way])
            place_ = major[flow][(UP, DOWN)[way]]
            rows = pl.ds(32 * way, 32)
            ps[flow, place_, :, rows, :] = (
                ps[flow, place_, :, rows, :].astype(F32) + ra[flow, way].astype(F32)
            ).astype(BF16)
            sum_send(flow, 2 + way, ps.at[flow, place_], rb.at[flow, way], 0, way)

    def gathered(flow, place_):
        return (
            ps[flow, major[flow][SELF], place_].astype(F32)
            + rb[flow, 0, place_].astype(F32)
            + rb[flow, 1, place_].astype(F32)
        )

    terms(1 - xl, y_far)
    terms(xl, y_far)
    far_out(0)
    terms(xl, y)
    terms(xl, y_up)
    terms(xl, y_down)
    far_out(1)
    terms(1 - xl, y_up)
    terms(1 - xl, y_down)
    terms(1 - xl, y)
    near_out(0)
    near_out(1)
    for flow in (0, 1):
        for way in (0, 1):
            sum_wait(flow, 2 + way, rb.at[flow, way])
        ta[flow, FAR] = gathered(flow, major[1 - flow][FAR]).astype(BF16)
        for way in (0, 1):
            src = ta.at[flow, FAR, pl.ds(32 * way, 32), :]
            sum_send(flow, 4 + way, src, rc.at[flow, way], 1, way)
    mine_sum = [gathered(flow, major[1 - flow][SELF]) for flow in (0, 1)]
    for flow in (0, 1):
        for way in (0, 1):
            near = gathered(flow, major[1 - flow][(UP, DOWN)[way]])
            sum_wait(flow, 4 + way, rc.at[flow, way])
            extra = rc[flow, way].astype(F32)
            if way == 0:
                near = jnp.concatenate([near[0:32] + extra, near[32:64]], axis=0)
            else:
                near = jnp.concatenate([near[0:32], near[32:64] + extra], axis=0)
            ta[flow, (UP, DOWN)[way]] = near.astype(BF16)
            sum_send(flow, 6 + way, ta.at[flow, (UP, DOWN)[way]], rd.at[flow, way], 1, way)
    for flow in (0, 1):
        rows = pl.ds(64 * flow, 64)
        whole = mine_sum[flow]
        for way in (0, 1):
            sum_wait(flow, 6 + way, rd.at[flow, way])
            whole = whole + rd[flow, way].astype(F32)
        ffn, ffn_d = whole[:, 0:WIDE], whole[:, WIDE:]
        out_ref[rows, :] = (ys[0, rows, :] + mod[3:4] * ffn).astype(BF16)
        outt_ref[rows, :] = (ys[1, rows, :] + modt[3:4] * ffn + mod[3:4] * ffn_d).astype(BF16)

    def drain(k, _):
        a1(k).wait_send()
        b1(k).wait_send()
        stat(k).wait_send()
        return 0

    lax.fori_loop(1, 16, drain, 0)
    for copy in kv_sends + b2_sends + block_sends + sum_sends + ring_sends + [to_ring, swap, share]:
        copy.wait_send()


def local(
    hidden_in, hidden_tan, query_in, key_in, value_in, query_tan, key_tan, value_tan,
    output_weight, feed_in, feed_out, modulation, modulation_tan, valid_rows, first_frame,
):
    vmem = pl.BlockSpec(memory_space=pltpu.VMEM)
    hbm = pl.BlockSpec(memory_space=pl.ANY)
    dma = pltpu.SemaphoreType.DMA
    shape = jax.ShapeDtypeStruct((ROWS, WIDE), BF16)
    return pl.pallas_call(
        kernel,
        out_shape=(shape, shape),
        in_specs=[pl.BlockSpec(memory_space=pltpu.SMEM)] + [vmem] * 3 + [hbm] * 11,
        out_specs=(vmem, vmem),
        scratch_shapes=[
            pltpu.VMEM((6, SUB, 4096), BF16),
            pltpu.VMEM((6, 2048, HD), BF16),
            pltpu.VMEM((256, 2048), F32),
            pltpu.VMEM((256, 2048), F32),
            pltpu.VMEM((256, 2048), BF16),
            pltpu.VMEM((256, 2048), BF16),
            pltpu.VMEM((2, 256, HD), BF16),
            pltpu.VMEM((2, 2, ROWS, 2048), BF16),
            pltpu.VMEM((2, ROWS, 384), BF16),
            pltpu.VMEM((WIDE, 4096), BF16),
            pltpu.VMEM((2, WIDE, HID), BF16),
            pltpu.VMEM((WIDE, PACK), BF16),
            pltpu.VMEM((8, WIDE, PACK), BF16),
            pltpu.VMEM((2, ROWS, WIDE), F32),
            pltpu.VMEM((16, 8, ROWS), F32),
            pltpu.VMEM((16, ROWS, 2 * WIDE), BF16),
            pltpu.VMEM((4 * ROWS, HID), F32),
            pltpu.VMEM((2 * ROWS, HID), F32),
            pltpu.VMEM((4 * ROWS, 512), BF16),
            pltpu.VMEM((2, 4, 4, 64, 2 * WIDE), BF16),
            pltpu.VMEM((2, 2, 4, 32, 2 * WIDE), BF16),
            pltpu.VMEM((2, 2, 4, 64, 2 * WIDE), BF16),
            pltpu.VMEM((2, 4, 64, 2 * WIDE), BF16),
            pltpu.VMEM((2, 2, 32, 2 * WIDE), BF16),
            pltpu.VMEM((2, 2, 64, 2 * WIDE), BF16),
            dma((11,)),
            dma((2,)),
            dma((16,)),
            dma((16,)),
            dma((8,)),
            dma((8,)),
            dma((8,)),
            dma((4, 2)),
            dma((16,)),
            dma((16,)),
            dma((17,)),
            dma((16,)),
            dma((16,)),
            dma((16,)),
            dma((2, 20)),
            dma((2, 16)),
            dma((4,)),
            dma((2, 8)),
            dma((2, 8)),
        ],
        compiler_params=pltpu.CompilerParams(
            collective_id=0, has_side_effects=True, vmem_limit_bytes=56 * 1024 * 1024
        ),
        cost_estimate=pl.CostEstimate(flops=4_000_000_000, bytes_accessed=20_000_000, transcendentals=1_000_000),
    )(
        first_frame, valid_rows.reshape(16, ROWS), modulation, modulation_tan,
        hidden_in, hidden_tan, query_in, key_in, value_in, query_tan, key_tan, value_tan,
        output_weight.T, feed_in, feed_out.T,
    )


def solution(mesh):
    rows = P("seq", None)
    placed = (rows,) * 8 + (P(None, "tp"), P("seq", "tp"), P("tp", "seq"), P(), P(), P(), P())
    return jax.shard_map(
        local, mesh=mesh, in_specs=placed, out_specs=(P("seq", "tp"), P("seq", "tp")), check_vma=False
    )
```

```python
import jax
import jax.numpy as jnp
from jax import lax
from jax.experimental import pallas as pl
from jax.experimental.pallas import tpu as pltpu
from jax.sharding import PartitionSpec as P

D = 5120
HD = 128
WIDE = 320
HID = 432
PACK = 896
ROWS = 128
SUB = 16
F32 = jnp.float32
BF16 = jnp.bfloat16
MESH = pl.DeviceIdType.MESH


def rem(a, b):
    return lax.rem(a, jnp.int32(b))


def div(a, b):
    return lax.div(a, jnp.int32(b))


def remote(src, dst, send, recv, device):
    return pltpu.make_async_remote_copy(
        src_ref=src, dst_ref=dst, send_sem=send, recv_sem=recv, device_id=device, device_id_type=MESH
    )


def dot_rows(a, b):
    return lax.dot_general(a, b, (((1,), (1,)), ((), ())), preferred_element_type=F32)


def kernel(
    first_ref, valid_ref, mod_ref, modt_ref,
    hid, hidt, q_in, k_in, v_in, q_tan, k_tan, v_tan, wo, w1, w2,
    out_ref, outt_ref,
    x6, grp, sc, dsc, pb, dpb, ao, at, hs, wob, wload, wown, wg, ys, st, hb, pre, prex, act,
    ps, ra, rb, ta, rc, rd,
    lsem, wsem, a1s, a1r, kvs, kvr, wr, ws, b1s, b1r, b2s, b2r, sts, str_, ds, dr, px, es, er,
):
    s = lax.axis_index("seq")
    t = lax.axis_index("tp")
    z, xh = div(s, 2), rem(s, 2)
    xl, y, c = div(t, 8), rem(div(t, 2), 4), rem(t, 2)
    x = 2 * xh + xl
    hf = rem(xl + xh, 2)
    yc = rem(t, 8)
    j = div(t, 2)
    plane = x * 4 + y
    sib = (s, t + 1 - 2 * c)

    def group(i):
        return (i, (rem(hf + rem(i, 2), 2) * 4 + y) * 2 + c)

    def chip(xx, yy):
        return (2 * z + div(xx, 2), (rem(xx, 2) * 4 + yy) * 2 + c)

    partner = (2 * z + c, ((1 - xl) * 4 + y) * 2 + xh)
    up, down = (rem(s + 2, 16), t), (rem(s + 14, 16), t)

    bar = pltpu.get_barrier_semaphore()

    def greet(k, _):
        pl.semaphore_signal(bar, inc=1, device_id=group(rem(s + k, 16)), device_id_type=MESH)
        pl.semaphore_signal(bar, inc=1, device_id=(s, rem(t + k, 16)), device_id_type=MESH)
        return 0

    lax.fori_loop(1, 16, greet, 0)
    pl.semaphore_signal(bar, inc=1, device_id=partner, device_id_type=MESH)

    my_rows = pl.ds(pl.multiple_of(yc * SUB, SUB), SUB)
    streams = (q_in, q_tan, k_in, k_tan, v_in, v_tan)

    def load(n):
        return pltpu.make_async_copy(streams[n].at[my_rows, :], x6.at[n], lsem.at[n])

    for n in range(6):
        load(n).start()
    load_w1 = pltpu.make_async_copy(w1, wload.at[0], lsem.at[9])
    load_w2 = pltpu.make_async_copy(w2, wload.at[1], lsem.at[10])
    load_w1.start()
    load_w2.start()
    start = pl.multiple_of(640 * j + 256 * c, 128)
    window = pl.ds(start, 384)
    load_h = pltpu.make_async_copy(hid.at[:, window], hs.at[0], lsem.at[6])
    load_ht = pltpu.make_async_copy(hidt.at[:, window], hs.at[1], lsem.at[7])
    load_wo = pltpu.make_async_copy(wo, wob, lsem.at[8])
    load_h.start()
    load_ht.start()
    load_wo.start()

    for n in range(6):
        load(n).wait()
    first = first_ref[0]
    place = s * ROWS + yc * SUB + lax.broadcasted_iota(jnp.int32, (SUB, 1), 0)
    keep_sub = place >= first
    for n in (1, 3, 5):
        x6[n] = jnp.where(keep_sub, x6[n].astype(F32), 0.0).astype(BF16)
    load_w1.wait()
    load_w2.wait()
    wown[:, 0:HID] = wload[0]
    wown[:, HID : 2 * HID] = wload[1]
    wown[:, 2 * HID :] = jnp.zeros((WIDE, PACK - 2 * HID), BF16)
    pl.semaphore_wait(bar, 31)

    def head_cols(i):
        head = div(i, 2) * 4 + 2 * hf + rem(i, 2)
        return pl.ds(pl.multiple_of(head * HD, HD), HD)

    def sub_of(i):
        return pl.ds(pl.multiple_of(yc * 256 + i * SUB, SUB), SUB)

    def owner(n):
        return rem(s + 24 + (1 - 2 * rem(n, 2)) * div(n + 1, 2), 16)

    def a1(pair, n):
        i = owner(n)
        src = x6.at[pl.ds(2 * pair, 2), :, head_cols(i)]
        return remote(src, grp.at[pl.ds(2 * pair, 2), sub_of(s), :], a1s.at[pair, n], a1r.at[pair, s], group(i))

    def a1_own(pair):
        src = x6.at[pl.ds(2 * pair, 2), :, head_cols(s)]
        return pltpu.make_async_copy(src, grp.at[pl.ds(2 * pair, 2), sub_of(s), :], a1r.at[pair, s])

    def a1_wait(pair):
        a1_own(pair).wait()

        def step(n, _):
            i = owner(n)
            dst = grp.at[pl.ds(2 * pair, 2), sub_of(i), :]
            remote(dst, dst, a1s.at[pair, n], a1r.at[pair, i], group(i)).wait_recv()
            return 0

        lax.fori_loop(0, 15, step, 0)

    QUERY, KEY, VALUE = range(3)
    for pair in (KEY, QUERY, VALUE):

        def a1_send(n, _):
            a1(pair, n).start()
            return 0

        lax.fori_loop(0, 15, a1_send, 0)
        a1_own(pair).start()

    to_ring = remote(wown, wg.at[z], wsem.at[0], wsem.at[1], partner)
    to_ring.start()
    ring_sends = []

    def ring(slot, step, way):
        view = wg.at[slot]
        if step == 3:
            view = view.at[pl.ds((0, WIDE // 2)[way], WIDE // 2), :]
        return remote(view, view, ws.at[step, way], wr.at[slot], (up, down)[way])

    def ring_wait(slot):
        ring(slot, 0, 0).wait_recv()

    def relay(step):
        below, above = rem(z + 8 - step, 8), rem(z + step, 8)
        if step > 0:
            ring_wait(below)
            ring_wait(above)
        for copy in (ring(below, step, 0), ring(above, step, 1)):
            copy.start()
            ring_sends.append(copy)

    def slot_rows(slot):
        return pl.ds(pl.multiple_of(slot * 256, 256), 256)

    def kv(pair, slot, n, device, low=0, count=2):
        view = grp.at[pl.ds(2 + 2 * pair + low, count), slot_rows(slot), :]
        return remote(view, view, kvs.at[pair, n], kvr.at[pair, slot], device)

    y_up, y_down, y_far = rem(y + 1, 4), rem(y + 3, 4), rem(y + 2, 4)
    x_up, x_down, x_far = rem(x + 1, 4), rem(x + 3, 4), rem(x + 2, 4)

    def column(yy):
        return (s, (xl * 4 + yy) * 2 + c)

    def same(yy):
        return yy * 2 + c

    def other(yy):
        return yy * 2 + 1 - c

    def kv_moves(pair):
        return [
            kv(pair, yc, 0, column(y_up)),
            kv(pair, yc, 1, column(y_down)),
            kv(pair, yc, 2, sib),
            kv(pair, same(y_down), 3, column(y_up), 0, 1),
            kv(pair, same(y_down), 4, sib),
            kv(pair, same(y_up), 5, column(y_down), 1, 1),
            kv(pair, same(y_up), 6, sib),
            kv(pair, same(y_far), 7, sib),
        ]

    kv_sends = kv_moves(0) + kv_moves(1)

    def kv_wait(pair, slot):
        kv(pair, slot, 0, sib).wait_recv()

    def kv_near(pair):
        kv_wait(pair, same(y_down))
        kv_sends[8 * pair + 3].start()
        kv_sends[8 * pair + 4].start()
        kv_wait(pair, same(y_up))
        kv_sends[8 * pair + 5].start()
        kv_sends[8 * pair + 6].start()

    def kv_far(pair):
        kv_wait(pair, same(y_far))
        kv_sends[8 * pair + 7].start()

    a1_wait(KEY)
    for copy in kv_sends[0:3]:
        copy.start()
    a1_wait(QUERY)

    factor = HD ** (-0.5)
    own = slot_rows(yc)
    valid = valid_ref[...].astype(F32).astype(BF16)
    from_lane = lax.broadcasted_iota(jnp.int32, (ROWS, 256), 0)
    to_lane = lax.broadcasted_iota(jnp.int32, (ROWS, 256), 1)
    shard_line = lax.broadcasted_iota(jnp.int32, (16, 256), 0)
    shard_lane = div(lax.broadcasted_iota(jnp.int32, (16, 256), 1), SUB)

    def score(slot):
        rows = slot_rows(slot)
        pick = jnp.where(from_lane == slot * SUB + rem(to_lane, SUB), 1.0, 0.0).astype(BF16)
        spread = jnp.dot(valid, pick, preferred_element_type=F32)
        allowed = jnp.sum(jnp.where(shard_line == shard_lane, spread, 0.0), axis=0, keepdims=True) > 0.5
        query = grp[0, own, :]
        keyed = grp[2, rows, :]
        both_q = jnp.concatenate([grp[1, own, :], query], axis=1)
        both_k = jnp.concatenate([keyed, grp[3, rows, :]], axis=1)
        sc[:, rows] = jnp.where(allowed, dot_rows(query, keyed) * factor, -1e30)
        dsc[:, rows] = jnp.where(allowed, dot_rows(both_q, both_k) * factor, 0.0)

    score(yc)
    kv_wait(0, other(y))
    score(other(y))
    kv_near(0)
    score(same(y_down))
    score(same(y_up))
    a1_wait(VALUE)
    for copy in kv_sends[8:11]:
        copy.start()
    to_ring.wait_recv()
    relay(0)
    kv_wait(0, other(y_down))
    score(other(y_down))
    kv_wait(0, other(y_up))
    score(other(y_up))
    kv_far(0)
    score(same(y_far))
    kv_wait(0, other(y_far))
    score(other(y_far))
    kv_near(1)

    def sixteen(n):
        return pl.ds(pl.multiple_of(n * SUB, SUB), SUB)

    def soft(n, _):
        rows, turned = sixteen(owner(n)), sixteen(n)
        values = sc[rows, :]
        expo = jnp.exp(values - jnp.max(values, axis=-1, keepdims=True))
        probs = expo * (1.0 / jnp.sum(expo, axis=-1, keepdims=True))
        tangent = dsc[rows, :]
        mean = jnp.sum(probs * tangent, axis=-1, keepdims=True)
        pb[turned, :] = probs.astype(BF16)
        dpb[turned, :] = (probs * (tangent - mean)).astype(BF16)
        return 0

    def weigh(half):
        rows = slice(128 * half, 128 * half + 128)
        both = jnp.dot(pb[rows, :], jnp.concatenate([grp[4], grp[5]], axis=1), preferred_element_type=F32)
        tangent = jnp.dot(dpb[rows, :], grp[4], preferred_element_type=F32)
        ao[0, rows, :] = both[:, 0:HD].astype(BF16)
        ao[1, rows, :] = (tangent + both[:, HD:]).astype(BF16)

    def seq_cols(i):
        return pl.ds(pl.multiple_of(i * HD, HD), HD)

    def b1(n):
        return remote(
            ao.at[:, sixteen(n), :], at.at[hf, :, my_rows, seq_cols(s)], b1s.at[n], b1r.at[s], group(owner(n))
        )

    def b1_send(n, _):
        b1(n).start()
        return 0

    lax.fori_loop(0, 8, soft, 0)
    kv_far(1)
    for yy in (y, y_down, y_up, y_far):
        kv_wait(1, other(yy))
    weigh(0)
    lax.fori_loop(0, 8, b1_send, 0)
    lax.fori_loop(8, 16, soft, 0)
    weigh(1)
    lax.fori_loop(8, 15, b1_send, 0)
    b1_own = pltpu.make_async_copy(ao.at[:, 240:256, :], at.at[hf, :, my_rows, seq_cols(s)], b1r.at[s])
    b1_own.start()
    b1_own.wait()

    def b1_wait(k, _):
        i = rem(s + k, 16)
        remote(
            ao.at[:, sixteen(0), :], at.at[hf, :, my_rows, seq_cols(i)], b1s.at[0], b1r.at[i], group(i)
        ).wait_recv()
        return 0

    lax.fori_loop(1, 16, b1_wait, 0)

    relay(1)

    def piece(xx, cc, n, device, low=0, count=2):
        rows = pl.ds(pl.multiple_of(cc * SUB, SUB), SUB)
        view = at.at[rem(xx + xh, 2), pl.ds(low, count), rows, :]
        return remote(view, view, b2s.at[n], b2r.at[xx * 8 + cc], device)

    def piece_wait(xx, cc):
        piece(xx, cc, 0, sib).wait_recv()

    across = (s, ((1 - xl) * 4 + y) * 2 + c)
    b2_sends = [
        piece(xl, yc, 0, across),
        piece(xl, yc, 1, column(y_up)),
        piece(xl, yc, 2, column(y_down)),
        piece(xl, yc, 3, sib),
        piece(1 - xl, yc, 4, column(y_up)),
        piece(1 - xl, yc, 5, column(y_down)),
        piece(1 - xl, yc, 6, sib),
    ]
    for n, xx in enumerate((xl, 1 - xl)):
        b2_sends += [
            piece(xx, same(y_down), 7 + 5 * n, column(y_up), 0, 1),
            piece(xx, same(y_down), 8 + 5 * n, sib),
            piece(xx, same(y_up), 9 + 5 * n, column(y_down), 1, 1),
            piece(xx, same(y_up), 10 + 5 * n, sib),
            piece(xx, same(y_far), 11 + 5 * n, sib),
        ]
    for copy in b2_sends[0:4]:
        copy.start()
    piece_wait(1 - xl, yc)
    for copy in b2_sends[4:7]:
        copy.start()
    for n, xx in enumerate((xl, 1 - xl)):
        piece_wait(xx, same(y_down))
        b2_sends[7 + 5 * n].start()
        b2_sends[8 + 5 * n].start()
        piece_wait(xx, same(y_up))
        b2_sends[9 + 5 * n].start()
        b2_sends[10 + 5 * n].start()
    for n, xx in enumerate((xl, 1 - xl)):
        piece_wait(xx, same(y_far))
        b2_sends[11 + 5 * n].start()
    for xx in (xl, 1 - xl):
        for yy in (y, y_down, y_up, y_far):
            piece_wait(xx, other(yy))

    relay(2)

    load_wo.wait()
    pre[:, 0:WIDE] = jnp.zeros((4 * ROWS, WIDE), F32)

    def project(n, _):
        cols = pl.ds(pl.multiple_of(n * 256, 256), 256)
        total = pre[0:256, 0:WIDE]
        for half in (0, 1):
            heads = pl.ds(pl.multiple_of((4 * n + 2 * half) * HD, 256), 256)
            total += dot_rows(at[half, :, :, cols].reshape(256, 256), wob[:, heads])
        pre[0:256, 0:WIDE] = total
        return 0

    lax.fori_loop(0, 8, project, 0)

    def narrow(wide):
        return jnp.where(c == 0, wide[:, 0:WIDE], wide[:, 64 : 64 + WIDE])

    mod = narrow(mod_ref[:, window])
    modt = narrow(modt_ref[:, window])
    load_h.wait()
    load_ht.wait()
    keep = s * ROWS + lax.broadcasted_iota(jnp.int32, (ROWS, 1), 0) >= first
    proj = pre[0:ROWS, 0:WIDE].astype(BF16).astype(F32)
    proj_d = pre[ROWS : 2 * ROWS, 0:WIDE].astype(BF16).astype(F32)
    resid = narrow(hs[0].astype(F32)) + mod[0:1] * proj
    hid_d = jnp.where(keep, narrow(hs[1].astype(F32)), 0.0)
    resid_d = hid_d + modt[0:1] * proj + mod[0:1] * proj_d
    ys[0] = resid
    ys[1] = resid_d
    mean_i = jnp.mean(resid, axis=-1, keepdims=True)
    dmean_i = jnp.mean(resid_d, axis=-1, keepdims=True)
    cen = resid - mean_i
    square = jnp.sum(cen * cen, axis=-1, keepdims=True)
    cross = jnp.sum(cen * (resid_d - dmean_i), axis=-1, keepdims=True)
    lane = lax.broadcasted_iota(jnp.int32, (ROWS, ROWS), 1)
    packed = jnp.where(
        lane == 0, mean_i, jnp.where(lane == 1, dmean_i, jnp.where(lane == 2, square, cross))
    )
    st[t] = packed.T[0:8, :]

    def stat(k):
        return remote(st.at[t], st.at[t], sts.at[k], str_.at[t], (s, rem(t + k, 16)))

    def stat_send(k, _):
        stat(k).start()
        return 0

    lax.fori_loop(1, 16, stat_send, 0)

    def stat_wait(k, _):
        tt = rem(t + k, 16)
        remote(st.at[tt], st.at[tt], sts.at[k], str_.at[tt], (s, tt)).wait_recv()
        return 0

    lax.fori_loop(1, 16, stat_wait, 0)
    means, dmeans = st[:, 0, :], st[:, 1, :]
    mean_row = jnp.mean(means, axis=0, keepdims=True)
    dmean_row = jnp.mean(dmeans, axis=0, keepdims=True)
    off = means - mean_row
    var_row = (jnp.sum(st[:, 2, :], axis=0, keepdims=True) + WIDE * jnp.sum(off * off, axis=0, keepdims=True)) / D
    cov_row = (
        jnp.sum(st[:, 3, :], axis=0, keepdims=True)
        + WIDE * jnp.sum(off * (dmeans - dmean_row), axis=0, keepdims=True)
    ) / D
    inv_row = lax.rsqrt(var_row + 1e-06)
    bend_row = inv_row * inv_row * inv_row * cov_row
    line = lax.broadcasted_iota(jnp.int32, (ROWS, ROWS), 0)
    cols = jnp.where(
        line == 0, mean_row, jnp.where(line == 1, dmean_row, jnp.where(line == 2, inv_row, bend_row))
    ).T
    cen = resid - cols[:, 0:1]
    inv = cols[:, 2:3]
    normed = cen * inv
    normed_d = (resid_d - cols[:, 1:2]) * inv - cen * cols[:, 3:4]
    grow = 1.0 + mod[2:3]
    hb[plane, :, 0:WIDE] = (normed * grow + mod[1:2]).astype(BF16)
    hb[plane, :, WIDE:] = (normed_d * grow + normed * modt[2:3] + modt[1:2]).astype(BF16)

    axes = (((x, x_up, x_down, x_far), (y, y_up, y_down, y_far)), ((y, y_up, y_down, y_far), (x, x_up, x_down, x_far)))
    SELF, UP, DOWN, FAR = range(4)

    def at_chip(flow, first_place, second_place):
        a, b = axes[flow][0][first_place], axes[flow][1][second_place]
        return (a, b) if flow == 0 else (b, a)

    block_sends = []

    def block(flow, first_place, second_place, low=0, count=64):
        xx, yy = at_chip(flow, first_place, second_place)
        slot = xx * 4 + yy
        view = hb.at[slot, pl.ds(64 * flow + low, count), :]
        return lambda n, device: remote(view, view, ds.at[flow, n], dr.at[flow, slot], device)

    counts = [0, 0]

    def block_send(flow, made, device):
        copy = made(counts[flow], device)
        counts[flow] += 1
        copy.start()
        block_sends.append(copy)

    def block_wait(flow, first_place, second_place):
        block(flow, first_place, second_place)(0, sib).wait_recv()

    def beside(flow, first_place, second_place):
        return chip(*at_chip(flow, first_place, second_place))

    def spread_second(flow, first_place):
        for way in (UP, DOWN):
            block_send(flow, block(flow, first_place, SELF), beside(flow, SELF, way))

    def pass_second(flow, first_place):
        block_wait(flow, first_place, DOWN)
        block_send(flow, block(flow, first_place, DOWN, 0, 32), beside(flow, SELF, UP))
        block_wait(flow, first_place, UP)
        block_send(flow, block(flow, first_place, UP, 32, 32), beside(flow, SELF, DOWN))

    for flow in (0, 1):
        for way in (UP, DOWN):
            block_send(flow, block(flow, SELF, SELF), beside(flow, way, SELF))
    for flow in (0, 1):
        spread_second(flow, SELF)
    for flow in (0, 1):
        block_wait(flow, DOWN, SELF)
        block_send(flow, block(flow, DOWN, SELF, 0, 32), beside(flow, UP, SELF))
        block_wait(flow, UP, SELF)
        block_send(flow, block(flow, UP, SELF, 32, 32), beside(flow, DOWN, SELF))
    for flow in (0, 1):
        spread_second(flow, DOWN)
        spread_second(flow, UP)
    for flow in (0, 1):
        block_wait(flow, FAR, SELF)
        spread_second(flow, FAR)
    relay(3)
    for first_place in (SELF, DOWN, UP, FAR):
        for flow in (0, 1):
            pass_second(flow, first_place)

    def feed(arr, xx, yy):
        lanes = slice(WIDE * arr, WIDE * arr + WIDE)
        rows = jnp.concatenate([hb[xx * 4 + yy, :, lanes], hb[(xx + 2) * 4 + yy, :, lanes]], axis=0)
        return jnp.dot(rows, wg[xx * 4 + yy, :, 0:HID], preferred_element_type=F32)

    ring_wait(rem(z + 4, 8))
    for arr in (0, 1):
        part = slice(256 * arr, 256 * arr + 256)
        pre[part, :] = feed(arr, 1 - xl, y)
        pre[part, :] += feed(arr, 1 - xl, y_up)
        pre[part, :] += feed(arr, 1 - xl, y_down)
    for first_place in (SELF, DOWN, UP, FAR):
        for flow in (0, 1):
            block_wait(flow, first_place, FAR)

    def half_of(arr, core):
        return pl.ds(pl.multiple_of(256 * arr + 128 * core, 128), ROWS)

    def swap(arr):
        return remote(pre.at[half_of(arr, 1 - c), :], prex.at[arr], px.at[arr], px.at[2 + arr], sib)

    def share(arr, core):
        view = act.at[half_of(arr, core), :]
        return remote(view, view, px.at[4 + arr], px.at[6 + arr], sib)

    def keep_act(arr, values):
        act[half_of(arr, c), :] = jnp.concatenate(
            [jnp.zeros((ROWS, 48), BF16), values.astype(BF16), jnp.zeros((ROWS, 32), BF16)], axis=1
        )
        share(arr, c).start()

    for arr in (0, 1):
        part = slice(256 * arr, 256 * arr + 256)
        pre[part, :] += feed(arr, 1 - xl, y_far)

        def feed_step(yy, _):
            pre[part, :] += feed(arr, xl, yy)
            return 0

        lax.fori_loop(0, 4, feed_step, 0)
        swap(arr).start()
    root = 0.7978845608028654
    cube = 0.044715
    swap(0).wait_recv()
    before = pre[half_of(0, c), :] + prex[0]
    squared = before * before
    bent = jnp.tanh(root * (before + cube * squared * before))
    half = 0.5 * (1.0 + bent)
    keep_act(0, before * half)
    slope = half + 0.5 * before * (1.0 - bent * bent) * (root * (1.0 + 3.0 * cube * squared))
    swap(1).wait_recv()
    keep_act(1, slope * (pre[half_of(1, c), :] + prex[1]))
    share(0, 1 - c).wait_recv()
    share(1, 1 - c).wait_recv()

    def terms(xx, yy):
        parts = dot_rows(act[...], wg[xx * 4 + yy, :, PACK - 512 :]).astype(BF16)
        for ee in (0, 1):
            both = jnp.concatenate([parts[128 * ee : 128 * ee + 128], parts[256 + 128 * ee : 384 + 128 * ee]], axis=1)
            ps[0, yy, xx + 2 * ee] = both[0:64]
            ps[1, xx + 2 * ee, yy] = both[64:128]

    major = ((y, y_up, y_down, y_far), (x, x_up, x_down, x_far))
    toward = (
        ((chip(x, y_up), chip(x, y_down)), (chip(x_up, y), chip(x_down, y))),
        ((chip(x_up, y), chip(x_down, y)), (chip(x, y_up), chip(x, y_down))),
    )
    sum_sends = []

    def sum_send(flow, n, src, dst, phase, way):
        copy = remote(src, dst, es.at[flow, n], er.at[flow, n], toward[flow][phase][way])
        copy.start()
        sum_sends.append(copy)

    def sum_wait(flow, n, dst):
        remote(dst, dst, es.at[flow, n], er.at[flow, n], sib).wait_recv()

    def far_out(flow):
        for way in (0, 1):
            src = ps.at[flow, major[flow][FAR], :, pl.ds(32 * way, 32), :]
            sum_send(flow, way, src, ra.at[flow, way], 0, way)

    def plain_out(flow, way):
        place_ = major[flow][(UP, DOWN)[way]]
        rows = pl.ds(32 * (1 - way), 32)
        sum_send(flow, 2 + way, ps.at[flow, place_, :, rows, :], rb.at[flow, way, :, rows, :], 0, way)

    def near_out(flow):
        for way in (0, 1):
            sum_wait(flow, way, ra.at[flow, way])
            place_ = major[flow][(UP, DOWN)[way]]
            rows = pl.ds(32 * way, 32)
            ps[flow, place_, :, rows, :] = (
                ps[flow, place_, :, rows, :].astype(F32) + ra[flow, way].astype(F32)
            ).astype(BF16)
            sum_send(flow, 4 + way, ps.at[flow, place_, :, rows, :], rb.at[flow, way, :, rows, :], 0, way)

    def gathered(flow, place_):
        return (
            ps[flow, major[flow][SELF], place_].astype(F32)
            + rb[flow, 0, place_].astype(F32)
            + rb[flow, 1, place_].astype(F32)
        )

    terms(1 - xl, y_far)
    terms(xl, y_far)
    far_out(0)
    terms(xl, y)
    terms(xl, y_up)
    terms(xl, y_down)
    far_out(1)
    terms(1 - xl, y_up)
    plain_out(0, 0)
    terms(1 - xl, y_down)
    plain_out(0, 1)
    terms(1 - xl, y)
    plain_out(1, 0)
    plain_out(1, 1)
    near_out(0)
    near_out(1)
    for flow in (0, 1):
        for way in (0, 1):
            lower, upper = rb.at[flow, way, :, 0:32, :], rb.at[flow, way, :, 32:64, :]
            sum_wait(flow, 2 + way, (upper, lower)[way])
            sum_wait(flow, 4 + way, (lower, upper)[way])
        ta[flow, FAR] = gathered(flow, major[1 - flow][FAR]).astype(BF16)
        for way in (0, 1):
            src = ta.at[flow, FAR, pl.ds(32 * way, 32), :]
            sum_send(flow, 6 + way, src, rc.at[flow, way], 1, way)
        for way in (0, 1):
            ta[flow, (UP, DOWN)[way]] = gathered(flow, major[1 - flow][(UP, DOWN)[way]]).astype(BF16)
            rows = pl.ds(32 * (1 - way), 32)
            src = ta.at[flow, (UP, DOWN)[way], rows, :]
            sum_send(flow, 8 + way, src, rd.at[flow, way, rows, :], 1, way)
    mine_sum = [gathered(flow, major[1 - flow][SELF]) for flow in (0, 1)]
    for flow in (0, 1):
        for way in (0, 1):
            place_ = (UP, DOWN)[way]
            rows = pl.ds(32 * way, 32)
            sum_wait(flow, 6 + way, rc.at[flow, way])
            ta[flow, place_, rows, :] = (ta[flow, place_, rows, :].astype(F32) + rc[flow, way].astype(F32)).astype(BF16)
            sum_send(flow, 10 + way, ta.at[flow, place_, rows, :], rd.at[flow, way, rows, :], 1, way)
    done = []
    for flow in (0, 1):
        rows = pl.ds(64 * flow, 64)
        whole = mine_sum[flow]
        for way in (0, 1):
            lower, upper = rd.at[flow, way, 0:32, :], rd.at[flow, way, 32:64, :]
            sum_wait(flow, 8 + way, (upper, lower)[way])
            sum_wait(flow, 10 + way, (lower, upper)[way])
            whole = whole + rd[flow, way].astype(F32)
        ffn, ffn_d = whole[:, 0:WIDE], whole[:, WIDE:]
        done.append((ys[0, rows, :] + mod[3:4] * ffn, ys[1, rows, :] + modt[3:4] * ffn + mod[3:4] * ffn_d))
    out_ref[...] = jnp.concatenate([done[0][0], done[1][0]], axis=0).T.astype(BF16)
    outt_ref[...] = jnp.concatenate([done[0][1], done[1][1]], axis=0).T.astype(BF16)

    def drain(k, _):
        for pair in (KEY, QUERY, VALUE):
            a1(pair, k - 1).wait_send()
        b1(k - 1).wait_send()
        stat(k).wait_send()
        return 0

    lax.fori_loop(1, 16, drain, 0)
    for copy in kv_sends + b2_sends + block_sends + sum_sends + ring_sends + [to_ring]:
        copy.wait_send()
    for arr in (0, 1):
        swap(arr).wait_send()
        share(arr, c).wait_send()


def local(
    hidden_in, hidden_tan, query_in, key_in, value_in, query_tan, key_tan, value_tan,
    output_weight, feed_in, feed_out, modulation, modulation_tan, valid_rows, first_frame,
):
    vmem = pl.BlockSpec(memory_space=pltpu.VMEM)
    hbm = pl.BlockSpec(memory_space=pl.ANY)
    dma = pltpu.SemaphoreType.DMA
    shape = jax.ShapeDtypeStruct((WIDE, ROWS), BF16)
    out, out_d = pl.pallas_call(
        kernel,
        out_shape=(shape, shape),
        in_specs=[pl.BlockSpec(memory_space=pltpu.SMEM)] + [vmem] * 3 + [hbm] * 11,
        out_specs=(vmem, vmem),
        scratch_shapes=[
            pltpu.VMEM((6, SUB, 4096), BF16),
            pltpu.VMEM((6, 2048, HD), BF16),
            pltpu.VMEM((256, 2048), F32),
            pltpu.VMEM((256, 2048), F32),
            pltpu.VMEM((256, 2048), BF16),
            pltpu.VMEM((256, 2048), BF16),
            pltpu.VMEM((2, 256, HD), BF16),
            pltpu.VMEM((2, 2, ROWS, 2048), BF16),
            pltpu.VMEM((2, ROWS, 384), BF16),
            pltpu.VMEM((WIDE, 4096), BF16),
            pltpu.VMEM((2, WIDE, HID), BF16),
            pltpu.VMEM((WIDE, PACK), BF16),
            pltpu.VMEM((8, WIDE, PACK), BF16),
            pltpu.VMEM((2, ROWS, WIDE), F32),
            pltpu.VMEM((16, 8, ROWS), F32),
            pltpu.VMEM((16, ROWS, 2 * WIDE), BF16),
            pltpu.VMEM((4 * ROWS, HID), F32),
            pltpu.VMEM((2, ROWS, HID), F32),
            pltpu.VMEM((4 * ROWS, 512), BF16),
            pltpu.VMEM((2, 4, 4, 64, 2 * WIDE), BF16),
            pltpu.VMEM((2, 2, 4, 32, 2 * WIDE), BF16),
            pltpu.VMEM((2, 2, 4, 64, 2 * WIDE), BF16),
            pltpu.VMEM((2, 4, 64, 2 * WIDE), BF16),
            pltpu.VMEM((2, 2, 32, 2 * WIDE), BF16),
            pltpu.VMEM((2, 2, 64, 2 * WIDE), BF16),
            dma((11,)),
            dma((2,)),
            dma((3, 16)),
            dma((3, 16)),
            dma((2, 8)),
            dma((2, 8)),
            dma((8,)),
            dma((4, 2)),
            dma((16,)),
            dma((16,)),
            dma((17,)),
            dma((16,)),
            dma((16,)),
            dma((16,)),
            dma((2, 20)),
            dma((2, 16)),
            dma((8,)),
            dma((2, 12)),
            dma((2, 12)),
        ],
        compiler_params=pltpu.CompilerParams(
            collective_id=0, has_side_effects=True, vmem_limit_bytes=56 * 1024 * 1024
        ),
        cost_estimate=pl.CostEstimate(flops=4_000_000_000, bytes_accessed=20_000_000, transcendentals=1_000_000),
    )(
        first_frame, valid_rows.reshape(16, ROWS), modulation, modulation_tan,
        hidden_in, hidden_tan, query_in, key_in, value_in, query_tan, key_tan, value_tan,
        output_weight.T, feed_in, feed_out.T,
    )
    return out.T, out_d.T


def solution(mesh):
    rows = P("seq", None)
    placed = (rows,) * 8 + (P(None, "tp"), P("seq", "tp"), P("tp", "seq"), P(), P(), P(), P())
    return jax.shard_map(
        local, mesh=mesh, in_specs=placed, out_specs=(P("seq", "tp"), P("seq", "tp")), check_vma=False
    )
```

```python
import jax
import jax.numpy as jnp
from jax import lax
from jax.experimental import pallas as pl
from jax.experimental.pallas import tpu as pltpu
from jax.sharding import PartitionSpec as P

D = 5120
HD = 128
WIDE = 320
HID = 432
PACK = 896
ROWS = 128
SUB = 16
F32 = jnp.float32
BF16 = jnp.bfloat16
MESH = pl.DeviceIdType.MESH


def rem(a, b):
    return lax.rem(a, jnp.int32(b))


def div(a, b):
    return lax.div(a, jnp.int32(b))


def remote(src, dst, send, recv, device):
    return pltpu.make_async_remote_copy(
        src_ref=src, dst_ref=dst, send_sem=send, recv_sem=recv, device_id=device, device_id_type=MESH
    )


def dot_rows(a, b):
    return lax.dot_general(a, b, (((1,), (1,)), ((), ())), preferred_element_type=F32)


def kernel(
    first_ref, valid_hbm, mod_hbm, modt_hbm,
    hid, hidt, q_in, k_in, v_in, q_tan, k_tan, v_tan, wo, w1, w2,
    out_ref, outt_ref,
    x6, grp, sc, dsc, pb, dpb, ao, at, hs, wob, wload, wown, wg, ys, st, hb, pre, prex, act,
    ps, ra, rb, ta, rc, rd, valid_ref, mods,
    lsem, wsem, a1s, a1r, kvs, kvr, wr, ws, b1s, b1r, b2s, b2r, sts, str_, ds, dr, px, es, er,
):
    s = lax.axis_index("seq")
    t = lax.axis_index("tp")
    z, xh = div(s, 2), rem(s, 2)
    xl, y, c = div(t, 8), rem(div(t, 2), 4), rem(t, 2)
    x = 2 * xh + xl
    hf = rem(xl + xh, 2)
    yc = rem(t, 8)
    j = div(t, 2)
    plane = x * 4 + y
    sib = (s, t + 1 - 2 * c)

    def group(i):
        return (i, (rem(hf + rem(i, 2), 2) * 4 + y) * 2 + c)

    def mate(k):
        return (s, rem(t + 2 * k, 16))

    def chip(xx, yy):
        return (2 * z + div(xx, 2), (rem(xx, 2) * 4 + yy) * 2 + c)

    partner = (2 * z + c, ((1 - xl) * 4 + y) * 2 + xh)
    up, down = (rem(s + 2, 16), t), (rem(s + 14, 16), t)

    bar = pltpu.get_barrier_semaphore()

    def greet(k, _):
        pl.semaphore_signal(bar, inc=1, device_id=group(rem(s + k, 16)), device_id_type=MESH)
        return 0

    def greet_column(k, _):
        pl.semaphore_signal(bar, inc=1, device_id=mate(k), device_id_type=MESH)
        return 0

    lax.fori_loop(1, 16, greet, 0)
    lax.fori_loop(1, 8, greet_column, 0)
    pl.semaphore_signal(bar, inc=1, device_id=sib, device_id_type=MESH)
    pl.semaphore_signal(bar, inc=1, device_id=partner, device_id_type=MESH)

    my_rows = pl.ds(pl.multiple_of(yc * SUB, SUB), SUB)
    streams = (q_in, q_tan, k_in, k_tan, v_in, v_tan)

    def load(n):
        return pltpu.make_async_copy(streams[n].at[my_rows, :], x6.at[n], lsem.at[n])

    for n in range(6):
        load(n).start()
    load_w1 = pltpu.make_async_copy(w1, wload.at[0], lsem.at[9])
    load_w2 = pltpu.make_async_copy(w2, wload.at[1], lsem.at[10])
    load_w1.start()
    load_w2.start()
    start = pl.multiple_of(640 * j + 256 * c, 128)
    window = pl.ds(start, 384)
    load_h = pltpu.make_async_copy(hid.at[:, window], hs.at[0], lsem.at[6])
    load_ht = pltpu.make_async_copy(hidt.at[:, window], hs.at[1], lsem.at[7])
    def load_wo(n):
        lanes = pl.ds(256 * n, 256)
        return pltpu.make_async_copy(wo.at[:, lanes], wob.at[n % 2, :, pl.ds(256 * (n // 2), 256)], wsem.at[2 + n])

    load_mod = pltpu.make_async_copy(mod_hbm.at[:, window], mods.at[0], lsem.at[11])
    load_modt = pltpu.make_async_copy(modt_hbm.at[:, window], mods.at[1], lsem.at[12])
    load_valid = pltpu.make_async_copy(valid_hbm, valid_ref, lsem.at[13])
    load_valid.start()
    load_mod.start()
    load_modt.start()
    load_h.start()
    load_ht.start()
    for n in range(16):
        load_wo(n).start()

    for n in range(6):
        load(n).wait()
    first = first_ref[0]
    place = s * ROWS + yc * SUB + lax.broadcasted_iota(jnp.int32, (SUB, 1), 0)
    keep_sub = place >= first
    for n in (1, 3, 5):
        x6[n] = jnp.where(keep_sub, x6[n].astype(F32), 0.0).astype(BF16)
    load_w1.wait()
    load_w2.wait()
    wown[:, 0:HID] = wload[0]
    wown[:, HID : 2 * HID] = wload[1]
    wown[:, 2 * HID :] = jnp.zeros((WIDE, PACK - 2 * HID), BF16)
    pl.semaphore_wait(bar, 24)

    def head_cols(i):
        head = div(i, 2) * 4 + 2 * hf + rem(i, 2)
        return pl.ds(pl.multiple_of(head * HD, HD), HD)

    def sub_of(i):
        return pl.ds(pl.multiple_of(yc * 256 + i * SUB, SUB), SUB)

    def owner(n):
        return rem(s + 24 + (1 - 2 * rem(n, 2)) * div(n + 1, 2), 16)

    def a1(pair, n):
        i = owner(n)
        src = x6.at[pl.ds(2 * pair, 2), :, head_cols(i)]
        return remote(src, grp.at[pl.ds(2 * pair, 2), sub_of(s), :], a1s.at[pair, n], a1r.at[pair, s], group(i))

    def a1_own(pair):
        src = x6.at[pl.ds(2 * pair, 2), :, head_cols(s)]
        return pltpu.make_async_copy(src, grp.at[pl.ds(2 * pair, 2), sub_of(s), :], a1r.at[pair, s])

    def a1_wait(pair):
        a1_own(pair).wait()

        def step(n, _):
            i = owner(n)
            dst = grp.at[pl.ds(2 * pair, 2), sub_of(i), :]
            remote(dst, dst, a1s.at[pair, n], a1r.at[pair, i], group(i)).wait_recv()
            return 0

        lax.fori_loop(0, 15, step, 0)

    QUERY, KEY, VALUE = range(3)

    def a1_out(pair):
        def step(n, _):
            a1(pair, n).start()
            return 0

        lax.fori_loop(0, 15, step, 0)
        a1_own(pair).start()

    a1_out(KEY)
    a1_out(QUERY)
    a1_out(VALUE)

    to_ring = remote(wown, wg.at[z], wsem.at[0], wsem.at[1], partner)
    to_ring.start()
    ring_sends = []

    def ring(slot, step, way):
        view = wg.at[slot]
        if step == 3:
            view = view.at[pl.ds((0, WIDE // 2)[way], WIDE // 2), :]
        return remote(view, view, ws.at[step, way], wr.at[slot], (up, down)[way])

    def ring_wait(slot):
        ring(slot, 0, 0).wait_recv()

    def relay(step):
        below, above = rem(z + 8 - step, 8), rem(z + step, 8)
        if step > 0:
            ring_wait(below)
            ring_wait(above)
        for copy in (ring(below, step, 0), ring(above, step, 1)):
            copy.start()
            ring_sends.append(copy)

    def slot_rows(slot):
        return pl.ds(pl.multiple_of(slot * 256, 256), 256)

    def kv(pair, slot, n, device, low=0, count=2):
        view = grp.at[pl.ds(2 + 2 * pair + low, count), slot_rows(slot), :]
        return remote(view, view, kvs.at[pair, n], kvr.at[pair, slot], device)

    y_up, y_down, y_far = rem(y + 1, 4), rem(y + 3, 4), rem(y + 2, 4)
    x_up, x_down, x_far = rem(x + 1, 4), rem(x + 3, 4), rem(x + 2, 4)

    def column(yy):
        return (s, (xl * 4 + yy) * 2 + c)

    def same(yy):
        return yy * 2 + c

    def other(yy):
        return yy * 2 + 1 - c

    def kv_moves(pair):
        return [
            kv(pair, yc, 0, column(y_up)),
            kv(pair, yc, 1, column(y_down)),
            kv(pair, yc, 2, sib),
            kv(pair, same(y_down), 3, column(y_up), 0, 1),
            kv(pair, same(y_down), 4, sib),
            kv(pair, same(y_up), 5, column(y_down), 1, 1),
            kv(pair, same(y_up), 6, sib),
            kv(pair, same(y_far), 7, sib),
        ]

    kv_sends = kv_moves(0) + kv_moves(1)

    def kv_wait(pair, slot):
        kv(pair, slot, 0, sib).wait_recv()

    def kv_near(pair):
        kv_wait(pair, same(y_down))
        kv_sends[8 * pair + 3].start()
        kv_sends[8 * pair + 4].start()
        kv_wait(pair, same(y_up))
        kv_sends[8 * pair + 5].start()
        kv_sends[8 * pair + 6].start()

    def kv_far(pair):
        kv_wait(pair, same(y_far))
        kv_sends[8 * pair + 7].start()

    a1_wait(KEY)
    for copy in kv_sends[0:3]:
        copy.start()
    a1_wait(QUERY)

    factor = HD ** (-0.5)
    own = slot_rows(yc)
    load_valid.wait()
    valid = valid_ref[...].astype(F32).astype(BF16)
    from_lane = lax.broadcasted_iota(jnp.int32, (ROWS, 256), 0)
    to_lane = lax.broadcasted_iota(jnp.int32, (ROWS, 256), 1)
    shard_line = lax.broadcasted_iota(jnp.int32, (16, 256), 0)
    shard_lane = div(lax.broadcasted_iota(jnp.int32, (16, 256), 1), SUB)

    def score(slot):
        rows = slot_rows(slot)
        pick = jnp.where(from_lane == slot * SUB + rem(to_lane, SUB), 1.0, 0.0).astype(BF16)
        spread = jnp.dot(valid, pick, preferred_element_type=F32)
        allowed = jnp.sum(jnp.where(shard_line == shard_lane, spread, 0.0), axis=0, keepdims=True) > 0.5
        query = grp[0, own, :]
        keyed = grp[2, rows, :]
        both_q = jnp.concatenate([grp[1, own, :], query], axis=1)
        both_k = jnp.concatenate([keyed, grp[3, rows, :]], axis=1)
        sc[:, rows] = jnp.where(allowed, dot_rows(query, keyed) * factor, -1e30)
        dsc[:, rows] = jnp.where(allowed, dot_rows(both_q, both_k) * factor, 0.0)

    score(yc)
    kv_wait(0, other(y))
    score(other(y))
    kv_near(0)
    score(same(y_down))
    score(same(y_up))
    a1_wait(VALUE)
    for copy in kv_sends[8:11]:
        copy.start()
    to_ring.wait_recv()
    relay(0)
    kv_wait(0, other(y_down))
    score(other(y_down))
    kv_wait(0, other(y_up))
    score(other(y_up))
    kv_far(0)
    score(same(y_far))
    kv_wait(0, other(y_far))
    score(other(y_far))
    kv_near(1)

    def sixteen(n):
        return pl.ds(pl.multiple_of(n * SUB, SUB), SUB)

    def soft(n, _):
        rows, turned = sixteen(owner(n)), sixteen(n)
        values = sc[rows, :]
        expo = jnp.exp(values - jnp.max(values, axis=-1, keepdims=True))
        probs = expo * (1.0 / jnp.sum(expo, axis=-1, keepdims=True))
        tangent = dsc[rows, :]
        mean = jnp.sum(probs * tangent, axis=-1, keepdims=True)
        pb[turned, :] = probs.astype(BF16)
        dpb[turned, :] = (probs * (tangent - mean)).astype(BF16)
        return 0

    def weigh(half):
        rows = slice(128 * half, 128 * half + 128)
        both = jnp.dot(pb[rows, :], jnp.concatenate([grp[4], grp[5]], axis=1), preferred_element_type=F32)
        tangent = jnp.dot(dpb[rows, :], grp[4], preferred_element_type=F32)
        ao[0, rows, :] = both[:, 0:HD].astype(BF16)
        ao[1, rows, :] = (tangent + both[:, HD:]).astype(BF16)

    def seq_cols(i):
        return pl.ds(pl.multiple_of(i * HD, HD), HD)

    def b1(n):
        return remote(
            ao.at[:, sixteen(n), :], at.at[hf, :, my_rows, seq_cols(s)], b1s.at[n], b1r.at[s], group(owner(n))
        )

    def b1_send(n, _):
        b1(n).start()
        return 0

    lax.fori_loop(0, 8, soft, 0)
    kv_far(1)
    for yy in (y, y_down, y_up, y_far):
        kv_wait(1, other(yy))
    weigh(0)
    lax.fori_loop(0, 8, b1_send, 0)
    lax.fori_loop(8, 16, soft, 0)
    weigh(1)
    lax.fori_loop(8, 15, b1_send, 0)
    b1_own = pltpu.make_async_copy(ao.at[:, 240:256, :], at.at[hf, :, my_rows, seq_cols(s)], b1r.at[s])
    b1_own.start()
    b1_own.wait()

    def b1_wait(k, _):
        i = rem(s + k, 16)
        remote(
            ao.at[:, sixteen(0), :], at.at[hf, :, my_rows, seq_cols(i)], b1s.at[0], b1r.at[i], group(i)
        ).wait_recv()
        return 0

    lax.fori_loop(1, 16, b1_wait, 0)

    relay(1)

    def narrow(wide):
        return jnp.where(c == 0, wide[:, 0:WIDE], wide[:, 64 : 64 + WIDE])

    def piece(xx, cc, n, device, low=0, count=2):
        rows = pl.ds(pl.multiple_of(cc * SUB, SUB), SUB)
        view = at.at[rem(xx + xh, 2), pl.ds(low, count), rows, :]
        return remote(view, view, b2s.at[n], b2r.at[xx * 8 + cc], device)

    def piece_wait(xx, cc):
        piece(xx, cc, 0, sib).wait_recv()

    across = (s, ((1 - xl) * 4 + y) * 2 + c)
    b2_sends = [
        piece(xl, yc, 0, across),
        piece(xl, yc, 1, column(y_up)),
        piece(xl, yc, 2, column(y_down)),
        piece(xl, yc, 3, sib),
        piece(1 - xl, yc, 4, column(y_up)),
        piece(1 - xl, yc, 5, column(y_down)),
        piece(1 - xl, yc, 6, sib),
    ]
    for n, xx in enumerate((xl, 1 - xl)):
        b2_sends += [
            piece(xx, same(y_down), 7 + 5 * n, column(y_up), 0, 1),
            piece(xx, same(y_down), 8 + 5 * n, sib),
            piece(xx, same(y_up), 9 + 5 * n, column(y_down), 1, 1),
            piece(xx, same(y_up), 10 + 5 * n, sib),
            piece(xx, same(y_far), 11 + 5 * n, sib),
        ]
    for copy in b2_sends[0:4]:
        copy.start()
    piece_wait(1 - xl, yc)
    for copy in b2_sends[4:7]:
        copy.start()
    for n, xx in enumerate((xl, 1 - xl)):
        piece_wait(xx, same(y_down))
        b2_sends[7 + 5 * n].start()
        b2_sends[8 + 5 * n].start()
        piece_wait(xx, same(y_up))
        b2_sends[9 + 5 * n].start()
        b2_sends[10 + 5 * n].start()
    load_h.wait()
    load_ht.wait()
    load_mod.wait()
    load_modt.wait()
    keep = s * ROWS + lax.broadcasted_iota(jnp.int32, (ROWS, 1), 0) >= first
    ys[0] = narrow(hs[0].astype(F32))
    ys[1] = jnp.where(keep, narrow(hs[1].astype(F32)), 0.0)
    for n, xx in enumerate((xl, 1 - xl)):
        piece_wait(xx, same(y_far))
        b2_sends[11 + 5 * n].start()
    for n in range(16):
        load_wo(n).wait()

    def project(xx):
        for yy in (y, y_down, y_up, y_far):
            piece_wait(xx, other(yy))
        half = rem(xx + xh, 2)
        return dot_rows(at[half].reshape(256, 2048), wob[half])

    pre[0:256, 0:WIDE] = project(xl)
    relay(2)
    pre[0:256, 0:WIDE] += project(1 - xl)

    mod = narrow(mods[0])
    modt = narrow(mods[1])
    proj = pre[0:ROWS, 0:WIDE].astype(BF16).astype(F32)
    proj_d = pre[ROWS : 2 * ROWS, 0:WIDE].astype(BF16).astype(F32)
    resid = ys[0] + mod[0:1] * proj
    resid_d = ys[1] + modt[0:1] * proj + mod[0:1] * proj_d
    ys[0] = resid
    ys[1] = resid_d
    mean_i = jnp.mean(resid, axis=-1, keepdims=True)
    dmean_i = jnp.mean(resid_d, axis=-1, keepdims=True)
    cen = resid - mean_i
    square = jnp.sum(cen * cen, axis=-1, keepdims=True)
    cross = jnp.sum(cen * (resid_d - dmean_i), axis=-1, keepdims=True)
    lane = lax.broadcasted_iota(jnp.int32, (ROWS, ROWS), 1)
    packed = jnp.where(
        lane == 0, mean_i, jnp.where(lane == 1, dmean_i, jnp.where(lane == 2, square, cross))
    )
    st[8] = packed.T[0:8, :]
    stat_sib = remote(st.at[8], st.at[9], sts.at[0], str_.at[8], sib)
    stat_sib.start()
    stat_sib.wait_recv()
    st[j] = jnp.concatenate([st[8, 0:4, :], st[9, 0:4, :]], axis=0)

    def stat(k):
        return remote(st.at[j], st.at[j], sts.at[k], str_.at[j], mate(k))

    def stat_send(k, _):
        stat(k).start()
        return 0

    lax.fori_loop(1, 8, stat_send, 0)

    def stat_wait(k, _):
        jj = rem(j + k, 8)
        remote(st.at[jj], st.at[jj], sts.at[k], str_.at[jj], mate(k)).wait_recv()
        return 0

    lax.fori_loop(1, 8, stat_wait, 0)

    def stats(n):
        return jnp.concatenate([st[0:8, n, :], st[0:8, n + 4, :]], axis=0)

    means, dmeans = stats(0), stats(1)
    mean_row = jnp.mean(means, axis=0, keepdims=True)
    dmean_row = jnp.mean(dmeans, axis=0, keepdims=True)
    off = means - mean_row
    var_row = (jnp.sum(stats(2), axis=0, keepdims=True) + WIDE * jnp.sum(off * off, axis=0, keepdims=True)) / D
    cov_row = (
        jnp.sum(stats(3), axis=0, keepdims=True)
        + WIDE * jnp.sum(off * (dmeans - dmean_row), axis=0, keepdims=True)
    ) / D
    inv_row = lax.rsqrt(var_row + 1e-06)
    bend_row = inv_row * inv_row * inv_row * cov_row
    line = lax.broadcasted_iota(jnp.int32, (ROWS, ROWS), 0)
    cols = jnp.where(
        line == 0, mean_row, jnp.where(line == 1, dmean_row, jnp.where(line == 2, inv_row, bend_row))
    ).T
    cen = resid - cols[:, 0:1]
    inv = cols[:, 2:3]
    normed = cen * inv
    normed_d = (resid_d - cols[:, 1:2]) * inv - cen * cols[:, 3:4]
    grow = 1.0 + mod[2:3]
    hb[plane, :, 0:WIDE] = (normed * grow + mod[1:2]).astype(BF16)
    hb[plane, :, WIDE:] = (normed_d * grow + normed * modt[2:3] + modt[1:2]).astype(BF16)

    axes = (((x, x_up, x_down, x_far), (y, y_up, y_down, y_far)), ((y, y_up, y_down, y_far), (x, x_up, x_down, x_far)))
    SELF, UP, DOWN, FAR = range(4)

    def at_chip(flow, first_place, second_place):
        a, b = axes[flow][0][first_place], axes[flow][1][second_place]
        return (a, b) if flow == 0 else (b, a)

    block_sends = []

    def block(flow, first_place, second_place, low=0, count=64):
        xx, yy = at_chip(flow, first_place, second_place)
        slot = xx * 4 + yy
        view = hb.at[slot, pl.ds(64 * flow + low, count), :]
        return lambda n, device: remote(view, view, ds.at[flow, n], dr.at[flow, slot], device)

    counts = [0, 0]

    def block_send(flow, made, device):
        copy = made(counts[flow], device)
        counts[flow] += 1
        copy.start()
        block_sends.append(copy)

    def block_wait(flow, first_place, second_place):
        block(flow, first_place, second_place)(0, sib).wait_recv()

    def beside(flow, first_place, second_place):
        return chip(*at_chip(flow, first_place, second_place))

    def spread_second(flow, first_place):
        for way in (UP, DOWN):
            block_send(flow, block(flow, first_place, SELF), beside(flow, SELF, way))

    def pass_second(flow, first_place):
        block_wait(flow, first_place, DOWN)
        block_send(flow, block(flow, first_place, DOWN, 0, 32), beside(flow, SELF, UP))
        block_wait(flow, first_place, UP)
        block_send(flow, block(flow, first_place, UP, 32, 32), beside(flow, SELF, DOWN))

    for flow in (0, 1):
        for way in (UP, DOWN):
            block_send(flow, block(flow, SELF, SELF), beside(flow, way, SELF))
    for flow in (0, 1):
        spread_second(flow, SELF)
    for flow in (0, 1):
        block_wait(flow, DOWN, SELF)
        block_send(flow, block(flow, DOWN, SELF, 0, 32), beside(flow, UP, SELF))
        block_wait(flow, UP, SELF)
        block_send(flow, block(flow, UP, SELF, 32, 32), beside(flow, DOWN, SELF))
    for flow in (0, 1):
        spread_second(flow, DOWN)
        spread_second(flow, UP)
    for flow in (0, 1):
        block_wait(flow, FAR, SELF)
        spread_second(flow, FAR)
    relay(3)
    for first_place in (SELF, DOWN, UP, FAR):
        for flow in (0, 1):
            pass_second(flow, first_place)

    def feed(arr, xx, yy):
        lanes = slice(WIDE * arr, WIDE * arr + WIDE)
        rows = jnp.concatenate([hb[xx * 4 + yy, :, lanes], hb[(xx + 2) * 4 + yy, :, lanes]], axis=0)
        return jnp.dot(rows, wg[xx * 4 + yy, :, 0:HID], preferred_element_type=F32)

    ring_wait(rem(z + 4, 8))
    for arr in (0, 1):
        part = slice(256 * arr, 256 * arr + 256)
        pre[part, :] = feed(arr, 1 - xl, y)
        pre[part, :] += feed(arr, 1 - xl, y_up)
        pre[part, :] += feed(arr, 1 - xl, y_down)
    for first_place in (SELF, DOWN, UP, FAR):
        for flow in (0, 1):
            block_wait(flow, first_place, FAR)

    def half_of(arr, core):
        return pl.ds(pl.multiple_of(256 * arr + 128 * core, 128), ROWS)

    def swap(arr):
        return remote(pre.at[half_of(arr, 1 - c), :], prex.at[arr], px.at[arr], px.at[2 + arr], sib)

    def share(arr, core):
        view = act.at[half_of(arr, core), :]
        return remote(view, view, px.at[4 + arr], px.at[6 + arr], sib)

    def keep_act(arr, values):
        act[half_of(arr, c), :] = jnp.concatenate(
            [jnp.zeros((ROWS, 48), BF16), values.astype(BF16), jnp.zeros((ROWS, 32), BF16)], axis=1
        )
        share(arr, c).start()

    for arr in (0, 1):
        part = slice(256 * arr, 256 * arr + 256)
        pre[part, :] += feed(arr, 1 - xl, y_far)

        def feed_step(yy, _):
            pre[part, :] += feed(arr, xl, yy)
            return 0

        lax.fori_loop(0, 4, feed_step, 0)
        swap(arr).start()
    root = 0.7978845608028654
    cube = 0.044715
    swap(0).wait_recv()
    before = pre[half_of(0, c), :] + prex[0]
    squared = before * before
    bent = jnp.tanh(root * (before + cube * squared * before))
    half = 0.5 * (1.0 + bent)
    keep_act(0, before * half)
    slope = half + 0.5 * before * (1.0 - bent * bent) * (root * (1.0 + 3.0 * cube * squared))
    swap(1).wait_recv()
    keep_act(1, slope * (pre[half_of(1, c), :] + prex[1]))
    share(0, 1 - c).wait_recv()
    share(1, 1 - c).wait_recv()

    def terms(*pair):
        weight = jnp.concatenate([wg[xx * 4 + yy, :, PACK - 512 :] for xx, yy in pair], axis=0)
        wide = dot_rows(act[...], weight).astype(BF16)
        for n, (xx, yy) in enumerate(pair):
            parts = wide[:, WIDE * n : WIDE * n + WIDE]
            for ee in (0, 1):
                both = jnp.concatenate(
                    [parts[128 * ee : 128 * ee + 128], parts[256 + 128 * ee : 384 + 128 * ee]], axis=1
                )
                ps[0, yy, xx + 2 * ee] = both[0:64]
                ps[1, xx + 2 * ee, yy] = both[64:128]

    major = ((y, y_up, y_down, y_far), (x, x_up, x_down, x_far))
    toward = (
        ((chip(x, y_up), chip(x, y_down)), (chip(x_up, y), chip(x_down, y))),
        ((chip(x_up, y), chip(x_down, y)), (chip(x, y_up), chip(x, y_down))),
    )
    sum_sends = []

    def sum_send(flow, n, src, dst, phase, way):
        copy = remote(src, dst, es.at[flow, n], er.at[flow, n], toward[flow][phase][way])
        copy.start()
        sum_sends.append(copy)

    def sum_wait(flow, n, dst):
        remote(dst, dst, es.at[flow, n], er.at[flow, n], sib).wait_recv()

    def far_out(flow):
        for way in (0, 1):
            src = ps.at[flow, major[flow][FAR], :, pl.ds(32 * way, 32), :]
            sum_send(flow, way, src, ra.at[flow, way], 0, way)

    def plain_out(flow, way):
        place_ = major[flow][(UP, DOWN)[way]]
        rows = pl.ds(32 * (1 - way), 32)
        sum_send(flow, 2 + way, ps.at[flow, place_, :, rows, :], rb.at[flow, way, :, rows, :], 0, way)

    def near_out(flow):
        for way in (0, 1):
            sum_wait(flow, way, ra.at[flow, way])
            place_ = major[flow][(UP, DOWN)[way]]
            rows = pl.ds(32 * way, 32)
            ps[flow, place_, :, rows, :] = (
                ps[flow, place_, :, rows, :].astype(F32) + ra[flow, way].astype(F32)
            ).astype(BF16)
            sum_send(flow, 4 + way, ps.at[flow, place_, :, rows, :], rb.at[flow, way, :, rows, :], 0, way)

    def gathered(flow, place_):
        return (
            ps[flow, major[flow][SELF], place_].astype(F32)
            + rb[flow, 0, place_].astype(F32)
            + rb[flow, 1, place_].astype(F32)
        )

    terms((1 - xl, y_far), (xl, y_far))
    far_out(0)
    terms((xl, y), (xl, y_up))
    terms((xl, y_down), (1 - xl, y_up))
    far_out(1)
    plain_out(0, 0)
    terms((1 - xl, y_down), (1 - xl, y))
    plain_out(0, 1)
    plain_out(1, 0)
    plain_out(1, 1)
    near_out(0)
    near_out(1)
    for flow in (0, 1):
        for way in (0, 1):
            lower, upper = rb.at[flow, way, :, 0:32, :], rb.at[flow, way, :, 32:64, :]
            sum_wait(flow, 2 + way, (upper, lower)[way])
            sum_wait(flow, 4 + way, (lower, upper)[way])
        ta[flow, FAR] = gathered(flow, major[1 - flow][FAR]).astype(BF16)
        for way in (0, 1):
            src = ta.at[flow, FAR, pl.ds(32 * way, 32), :]
            sum_send(flow, 6 + way, src, rc.at[flow, way], 1, way)
        for way in (0, 1):
            ta[flow, (UP, DOWN)[way]] = gathered(flow, major[1 - flow][(UP, DOWN)[way]]).astype(BF16)
            rows = pl.ds(32 * (1 - way), 32)
            src = ta.at[flow, (UP, DOWN)[way], rows, :]
            sum_send(flow, 8 + way, src, rd.at[flow, way, rows, :], 1, way)
    mine_sum = [gathered(flow, major[1 - flow][SELF]) for flow in (0, 1)]
    for flow in (0, 1):
        for way in (0, 1):
            place_ = (UP, DOWN)[way]
            rows = pl.ds(32 * way, 32)
            sum_wait(flow, 6 + way, rc.at[flow, way])
            ta[flow, place_, rows, :] = (ta[flow, place_, rows, :].astype(F32) + rc[flow, way].astype(F32)).astype(BF16)
            sum_send(flow, 10 + way, ta.at[flow, place_, rows, :], rd.at[flow, way, rows, :], 1, way)
    done = []
    for flow in (0, 1):
        rows = pl.ds(64 * flow, 64)
        whole = mine_sum[flow]
        for way in (0, 1):
            lower, upper = rd.at[flow, way, 0:32, :], rd.at[flow, way, 32:64, :]
            sum_wait(flow, 8 + way, (upper, lower)[way])
            sum_wait(flow, 10 + way, (lower, upper)[way])
            whole = whole + rd[flow, way].astype(F32)
        ffn, ffn_d = whole[:, 0:WIDE], whole[:, WIDE:]
        done.append((ys[0, rows, :] + mod[3:4] * ffn, ys[1, rows, :] + modt[3:4] * ffn + mod[3:4] * ffn_d))
    out_ref[...] = jnp.concatenate([done[0][0], done[1][0]], axis=0).T.astype(BF16)
    outt_ref[...] = jnp.concatenate([done[0][1], done[1][1]], axis=0).T.astype(BF16)

    def drain(k, _):
        for pair in (KEY, QUERY, VALUE):
            a1(pair, k - 1).wait_send()
        b1(k - 1).wait_send()
        return 0

    def drain_stat(k, _):
        stat(k).wait_send()
        return 0

    lax.fori_loop(1, 16, drain, 0)
    lax.fori_loop(1, 8, drain_stat, 0)
    stat_sib.wait_send()
    for copy in kv_sends + b2_sends + block_sends + sum_sends + ring_sends + [to_ring]:
        copy.wait_send()
    for arr in (0, 1):
        swap(arr).wait_send()
        share(arr, c).wait_send()


def local(
    hidden_in, hidden_tan, query_in, key_in, value_in, query_tan, key_tan, value_tan,
    output_weight, feed_in, feed_out, modulation, modulation_tan, valid_rows, first_frame,
):
    vmem = pl.BlockSpec(memory_space=pltpu.VMEM)
    hbm = pl.BlockSpec(memory_space=pl.ANY)
    dma = pltpu.SemaphoreType.DMA
    shape = jax.ShapeDtypeStruct((WIDE, ROWS), BF16)
    out, out_d = pl.pallas_call(
        kernel,
        out_shape=(shape, shape),
        in_specs=[pl.BlockSpec(memory_space=pltpu.SMEM)] + [hbm] * 14,
        out_specs=(vmem, vmem),
        scratch_shapes=[
            pltpu.VMEM((6, SUB, 4096), BF16),
            pltpu.VMEM((6, 2048, HD), BF16),
            pltpu.VMEM((256, 2048), F32),
            pltpu.VMEM((256, 2048), F32),
            pltpu.VMEM((256, 2048), BF16),
            pltpu.VMEM((256, 2048), BF16),
            pltpu.VMEM((2, 256, HD), BF16),
            pltpu.VMEM((2, 2, ROWS, 2048), BF16),
            pltpu.VMEM((2, ROWS, 384), BF16),
            pltpu.VMEM((2, WIDE, 2048), BF16),
            pltpu.VMEM((2, WIDE, HID), BF16),
            pltpu.VMEM((WIDE, PACK), BF16),
            pltpu.VMEM((8, WIDE, PACK), BF16),
            pltpu.VMEM((2, ROWS, WIDE), F32),
            pltpu.VMEM((10, 8, ROWS), F32),
            pltpu.VMEM((16, ROWS, 2 * WIDE), BF16),
            pltpu.VMEM((4 * ROWS, HID), F32),
            pltpu.VMEM((2, ROWS, HID), F32),
            pltpu.VMEM((4 * ROWS, 512), BF16),
            pltpu.VMEM((2, 4, 4, 64, 2 * WIDE), BF16),
            pltpu.VMEM((2, 2, 4, 32, 2 * WIDE), BF16),
            pltpu.VMEM((2, 2, 4, 64, 2 * WIDE), BF16),
            pltpu.VMEM((2, 4, 64, 2 * WIDE), BF16),
            pltpu.VMEM((2, 2, 32, 2 * WIDE), BF16),
            pltpu.VMEM((2, 2, 64, 2 * WIDE), BF16),
            pltpu.VMEM((16, ROWS), jnp.int32),
            pltpu.VMEM((2, 4, 384), F32),
            dma((14,)),
            dma((18,)),
            dma((3, 16)),
            dma((3, 16)),
            dma((2, 8)),
            dma((2, 8)),
            dma((8,)),
            dma((4, 2)),
            dma((16,)),
            dma((16,)),
            dma((17,)),
            dma((16,)),
            dma((16,)),
            dma((16,)),
            dma((2, 20)),
            dma((2, 16)),
            dma((8,)),
            dma((2, 12)),
            dma((2, 12)),
        ],
        compiler_params=pltpu.CompilerParams(
            collective_id=0, has_side_effects=True, vmem_limit_bytes=56 * 1024 * 1024
        ),
        cost_estimate=pl.CostEstimate(flops=4_000_000_000, bytes_accessed=20_000_000, transcendentals=1_000_000),
    )(
        first_frame, valid_rows.reshape(16, ROWS), modulation, modulation_tan,
        hidden_in, hidden_tan, query_in, key_in, value_in, query_tan, key_tan, value_tan,
        output_weight.T, feed_in, feed_out.T,
    )
    return out.T, out_d.T


def solution(mesh):
    rows = P("seq", None)
    placed = (rows,) * 8 + (P(None, "tp"), P("seq", "tp"), P("tp", "seq"), P(), P(), P(), P())
    return jax.shard_map(
        local, mesh=mesh, in_specs=placed, out_specs=(P("seq", "tp"), P("seq", "tp")), check_vma=False
    )
```

```python
import jax
import jax.numpy as jnp
from jax import lax
from jax.experimental import pallas as pl
from jax.experimental.pallas import tpu as pltpu
from jax.sharding import PartitionSpec as P

D = 5120
HD = 128
WIDE = 320
HID = 432
PACK = 896
ROWS = 128
SUB = 16
F32 = jnp.float32
BF16 = jnp.bfloat16
MESH = pl.DeviceIdType.MESH


def rem(a, b):
    return lax.rem(a, jnp.int32(b))


def div(a, b):
    return lax.div(a, jnp.int32(b))


def remote(src, dst, send, recv, device):
    return pltpu.make_async_remote_copy(
        src_ref=src, dst_ref=dst, send_sem=send, recv_sem=recv, device_id=device, device_id_type=MESH
    )


def dot_rows(a, b):
    return lax.dot_general(a, b, (((1,), (1,)), ((), ())), preferred_element_type=F32)


def kernel(
    first_ref, valid_hbm, mod_hbm, modt_hbm,
    hid, hidt, q_in, k_in, v_in, q_tan, k_tan, v_tan, wo, w1, w2,
    out_ref, outt_ref,
    x6, grp, sc, dsc, pb, dpb, ao, at, hs, wob, wload, wown, wg, ys, st, hb, pre, prex, act,
    ps, ra, rb, ta, rc, rd, valid_ref, mods,
    lsem, wsem, a1s, a1r, kvs, kvr, wr, ws, b1s, b1r, b2s, b2r, sts, str_, ds, dr, px, es, er,
):
    s = lax.axis_index("seq")
    t = lax.axis_index("tp")
    z, xh = div(s, 2), rem(s, 2)
    xl, y, c = div(t, 8), rem(div(t, 2), 4), rem(t, 2)
    x = 2 * xh + xl
    hf = rem(xl + xh, 2)
    yc = rem(t, 8)
    j = div(t, 2)
    plane = x * 4 + y
    sib = (s, t + 1 - 2 * c)

    def group(i):
        return (i, (rem(hf + rem(i, 2), 2) * 4 + y) * 2 + c)

    def mate(k):
        return (s, rem(t + 2 * k, 16))

    def chip(xx, yy):
        return (2 * z + div(xx, 2), (rem(xx, 2) * 4 + yy) * 2 + c)

    partner = (2 * z + c, ((1 - xl) * 4 + y) * 2 + xh)
    up, down = (rem(s + 2, 16), t), (rem(s + 14, 16), t)

    bar = pltpu.get_barrier_semaphore()

    def greet(k, _):
        pl.semaphore_signal(bar, inc=1, device_id=group(rem(s + k, 16)), device_id_type=MESH)
        return 0

    def greet_column(k, _):
        pl.semaphore_signal(bar, inc=1, device_id=mate(k), device_id_type=MESH)
        return 0

    lax.fori_loop(1, 16, greet, 0)
    lax.fori_loop(1, 8, greet_column, 0)
    pl.semaphore_signal(bar, inc=1, device_id=sib, device_id_type=MESH)
    pl.semaphore_signal(bar, inc=1, device_id=partner, device_id_type=MESH)

    my_rows = pl.ds(pl.multiple_of(yc * SUB, SUB), SUB)
    streams = (q_in, q_tan, k_in, k_tan, v_in, v_tan)

    def load(n):
        return pltpu.make_async_copy(streams[n].at[my_rows, :], x6.at[n], lsem.at[n])

    for n in range(6):
        load(n).start()
    load_w1 = pltpu.make_async_copy(w1, wload.at[0], lsem.at[9])
    load_w2 = pltpu.make_async_copy(w2, wload.at[1], lsem.at[10])
    load_w1.start()
    load_w2.start()
    start = pl.multiple_of(640 * j + 256 * c, 128)
    window = pl.ds(start, 384)
    load_h = pltpu.make_async_copy(hid.at[:, window], hs.at[0], lsem.at[6])
    load_ht = pltpu.make_async_copy(hidt.at[:, window], hs.at[1], lsem.at[7])
    def load_wo(n):
        lanes = pl.ds(256 * n, 256)
        return pltpu.make_async_copy(wo.at[:, lanes], wob.at[n % 2, :, pl.ds(256 * (n // 2), 256)], wsem.at[2 + n])

    load_mod = pltpu.make_async_copy(mod_hbm.at[:, window], mods.at[0], lsem.at[11])
    load_modt = pltpu.make_async_copy(modt_hbm.at[:, window], mods.at[1], lsem.at[12])
    load_valid = pltpu.make_async_copy(valid_hbm, valid_ref, lsem.at[13])
    load_valid.start()
    load_mod.start()
    load_modt.start()
    load_h.start()
    load_ht.start()
    for n in range(16):
        load_wo(n).start()

    for n in range(6):
        load(n).wait()
    first = first_ref[0]
    place = s * ROWS + yc * SUB + lax.broadcasted_iota(jnp.int32, (SUB, 1), 0)
    keep_sub = place >= first
    for n in (1, 3, 5):
        x6[n] = jnp.where(keep_sub, x6[n].astype(F32), 0.0).astype(BF16)
    load_w1.wait()
    load_w2.wait()
    wown[:, 0:HID] = wload[0]
    wown[:, HID : 2 * HID] = wload[1]
    wown[:, 2 * HID :] = jnp.zeros((WIDE, PACK - 2 * HID), BF16)
    pl.semaphore_wait(bar, 24)

    def head_cols(i):
        head = div(i, 2) * 4 + 2 * hf + rem(i, 2)
        return pl.ds(pl.multiple_of(head * HD, HD), HD)

    def sub_of(i):
        return pl.ds(pl.multiple_of(yc * 256 + i * SUB, SUB), SUB)

    def owner(n):
        return rem(s + 24 + (1 - 2 * rem(n, 2)) * div(n + 1, 2), 16)

    def a1(pair, n):
        i = owner(n)
        src = x6.at[pl.ds(2 * pair, 2), :, head_cols(i)]
        return remote(src, grp.at[pl.ds(2 * pair, 2), sub_of(s), :], a1s.at[pair, n], a1r.at[pair, s], group(i))

    def a1_own(pair):
        src = x6.at[pl.ds(2 * pair, 2), :, head_cols(s)]
        return pltpu.make_async_copy(src, grp.at[pl.ds(2 * pair, 2), sub_of(s), :], a1r.at[pair, s])

    def a1_wait(pair):
        a1_own(pair).wait()

        def step(n, _):
            i = owner(n)
            dst = grp.at[pl.ds(2 * pair, 2), sub_of(i), :]
            remote(dst, dst, a1s.at[pair, n], a1r.at[pair, i], group(i)).wait_recv()
            return 0

        lax.fori_loop(0, 15, step, 0)

    QUERY, KEY, VALUE = range(3)

    def a1_out(pair):
        def step(n, _):
            a1(pair, n).start()
            return 0

        lax.fori_loop(0, 15, step, 0)
        a1_own(pair).start()

    a1_out(KEY)
    a1_out(QUERY)
    to_ring = remote(wown, wg.at[z], wsem.at[0], wsem.at[1], partner)
    to_ring.start()
    a1_out(VALUE)

    ring_sends = []

    def ring(slot, step, way):
        view = wg.at[slot]
        if step == 3:
            view = view.at[pl.ds((0, WIDE // 2)[way], WIDE // 2), :]
        return remote(view, view, ws.at[step, way], wr.at[slot], (up, down)[way])

    def ring_wait(slot):
        ring(slot, 0, 0).wait_recv()

    def relay(step):
        below, above = rem(z + 8 - step, 8), rem(z + step, 8)
        if step > 0:
            ring_wait(below)
            ring_wait(above)
        for copy in (ring(below, step, 0), ring(above, step, 1)):
            copy.start()
            ring_sends.append(copy)

    def slot_rows(slot):
        return pl.ds(pl.multiple_of(slot * 256, 256), 256)

    def kv(pair, slot, n, device, low=0, count=2):
        view = grp.at[pl.ds(2 + 2 * pair + low, count), slot_rows(slot), :]
        return remote(view, view, kvs.at[pair, n], kvr.at[pair, slot], device)

    y_up, y_down, y_far = rem(y + 1, 4), rem(y + 3, 4), rem(y + 2, 4)
    x_up, x_down, x_far = rem(x + 1, 4), rem(x + 3, 4), rem(x + 2, 4)

    def column(yy):
        return (s, (xl * 4 + yy) * 2 + c)

    def same(yy):
        return yy * 2 + c

    def other(yy):
        return yy * 2 + 1 - c

    def kv_moves(pair):
        return [
            kv(pair, yc, 0, column(y_up)),
            kv(pair, yc, 1, column(y_down)),
            kv(pair, yc, 2, sib),
            kv(pair, same(y_down), 3, column(y_up), 0, 1),
            kv(pair, same(y_down), 4, sib),
            kv(pair, same(y_up), 5, column(y_down), 1, 1),
            kv(pair, same(y_up), 6, sib),
            kv(pair, same(y_far), 7, sib),
        ]

    kv_sends = kv_moves(0) + kv_moves(1)

    def kv_wait(pair, slot):
        kv(pair, slot, 0, sib).wait_recv()

    def kv_near(pair):
        kv_wait(pair, same(y_down))
        kv_sends[8 * pair + 3].start()
        kv_sends[8 * pair + 4].start()
        kv_wait(pair, same(y_up))
        kv_sends[8 * pair + 5].start()
        kv_sends[8 * pair + 6].start()

    def kv_far(pair):
        kv_wait(pair, same(y_far))
        kv_sends[8 * pair + 7].start()

    a1_wait(KEY)
    for copy in kv_sends[0:3]:
        copy.start()
    a1_wait(QUERY)

    factor = HD ** (-0.5)
    own = slot_rows(yc)
    load_valid.wait()
    valid = valid_ref[...].astype(F32).astype(BF16)
    from_lane = lax.broadcasted_iota(jnp.int32, (ROWS, 256), 0)
    to_lane = lax.broadcasted_iota(jnp.int32, (ROWS, 256), 1)
    shard_line = lax.broadcasted_iota(jnp.int32, (16, 256), 0)
    shard_lane = div(lax.broadcasted_iota(jnp.int32, (16, 256), 1), SUB)

    def score(slot):
        rows = slot_rows(slot)
        pick = jnp.where(from_lane == slot * SUB + rem(to_lane, SUB), 1.0, 0.0).astype(BF16)
        spread = jnp.dot(valid, pick, preferred_element_type=F32)
        allowed = jnp.sum(jnp.where(shard_line == shard_lane, spread, 0.0), axis=0, keepdims=True) > 0.5
        query = grp[0, own, :]
        keyed = grp[2, rows, :]
        both_q = jnp.concatenate([grp[1, own, :], query], axis=1)
        both_k = jnp.concatenate([keyed, grp[3, rows, :]], axis=1)
        sc[:, rows] = jnp.where(allowed, dot_rows(query, keyed) * factor, -1e30)
        dsc[:, rows] = jnp.where(allowed, dot_rows(both_q, both_k) * factor, 0.0)

    score(yc)
    kv_wait(0, other(y))
    score(other(y))
    kv_near(0)
    score(same(y_down))
    score(same(y_up))
    a1_wait(VALUE)
    for copy in kv_sends[8:11]:
        copy.start()
    to_ring.wait_recv()
    relay(0)
    kv_wait(0, other(y_down))
    score(other(y_down))
    kv_wait(0, other(y_up))
    score(other(y_up))
    kv_far(0)
    score(same(y_far))
    kv_wait(0, other(y_far))
    score(other(y_far))
    kv_near(1)

    def sixteen(n):
        return pl.ds(pl.multiple_of(n * SUB, SUB), SUB)

    def soft(n, _):
        rows, turned = sixteen(owner(n)), sixteen(n)
        values = sc[rows, :]
        expo = jnp.exp(values - jnp.max(values, axis=-1, keepdims=True))
        probs = expo * (1.0 / jnp.sum(expo, axis=-1, keepdims=True))
        tangent = dsc[rows, :]
        mean = jnp.sum(probs * tangent, axis=-1, keepdims=True)
        pb[turned, :] = probs.astype(BF16)
        dpb[turned, :] = (probs * (tangent - mean)).astype(BF16)
        return 0

    def weigh(half):
        rows = slice(128 * half, 128 * half + 128)
        both = jnp.dot(pb[rows, :], jnp.concatenate([grp[4], grp[5]], axis=1), preferred_element_type=F32)
        tangent = jnp.dot(dpb[rows, :], grp[4], preferred_element_type=F32)
        ao[0, rows, :] = both[:, 0:HD].astype(BF16)
        ao[1, rows, :] = (tangent + both[:, HD:]).astype(BF16)

    def seq_cols(i):
        return pl.ds(pl.multiple_of(i * HD, HD), HD)

    def b1(n):
        return remote(
            ao.at[:, sixteen(n), :], at.at[hf, :, my_rows, seq_cols(s)], b1s.at[n], b1r.at[s], group(owner(n))
        )

    def b1_send(n, _):
        b1(n).start()
        return 0

    lax.fori_loop(0, 8, soft, 0)
    kv_far(1)
    for yy in (y, y_down, y_up, y_far):
        kv_wait(1, other(yy))
    weigh(0)
    lax.fori_loop(0, 8, b1_send, 0)
    lax.fori_loop(8, 16, soft, 0)
    weigh(1)
    lax.fori_loop(8, 15, b1_send, 0)
    b1_own = pltpu.make_async_copy(ao.at[:, 240:256, :], at.at[hf, :, my_rows, seq_cols(s)], b1r.at[s])
    b1_own.start()
    b1_own.wait()

    def b1_wait(k, _):
        i = rem(s + k, 16)
        remote(
            ao.at[:, sixteen(0), :], at.at[hf, :, my_rows, seq_cols(i)], b1s.at[0], b1r.at[i], group(i)
        ).wait_recv()
        return 0

    lax.fori_loop(1, 16, b1_wait, 0)

    relay(1)

    def narrow(wide):
        return jnp.where(c == 0, wide[:, 0:WIDE], wide[:, 64 : 64 + WIDE])

    def piece(xx, cc, n, device, low=0, count=2):
        rows = pl.ds(pl.multiple_of(cc * SUB, SUB), SUB)
        view = at.at[rem(xx + xh, 2), pl.ds(low, count), rows, :]
        return remote(view, view, b2s.at[n], b2r.at[xx * 8 + cc], device)

    def piece_wait(xx, cc):
        piece(xx, cc, 0, sib).wait_recv()

    across = (s, ((1 - xl) * 4 + y) * 2 + c)
    b2_sends = [
        piece(xl, yc, 0, across),
        piece(xl, yc, 1, column(y_up)),
        piece(xl, yc, 2, column(y_down)),
        piece(xl, yc, 3, sib),
        piece(1 - xl, yc, 4, column(y_up)),
        piece(1 - xl, yc, 5, column(y_down)),
        piece(1 - xl, yc, 6, sib),
    ]
    for n, xx in enumerate((xl, 1 - xl)):
        b2_sends += [
            piece(xx, same(y_down), 7 + 5 * n, column(y_up), 0, 1),
            piece(xx, same(y_down), 8 + 5 * n, sib),
            piece(xx, same(y_up), 9 + 5 * n, column(y_down), 1, 1),
            piece(xx, same(y_up), 10 + 5 * n, sib),
            piece(xx, same(y_far), 11 + 5 * n, sib),
        ]
    for copy in b2_sends[0:4]:
        copy.start()
    piece_wait(1 - xl, yc)
    for copy in b2_sends[4:7]:
        copy.start()
    for n, xx in enumerate((xl, 1 - xl)):
        piece_wait(xx, same(y_down))
        b2_sends[7 + 5 * n].start()
        b2_sends[8 + 5 * n].start()
        piece_wait(xx, same(y_up))
        b2_sends[9 + 5 * n].start()
        b2_sends[10 + 5 * n].start()
    load_h.wait()
    load_ht.wait()
    load_mod.wait()
    load_modt.wait()
    keep = s * ROWS + lax.broadcasted_iota(jnp.int32, (ROWS, 1), 0) >= first
    ys[0] = narrow(hs[0].astype(F32))
    ys[1] = jnp.where(keep, narrow(hs[1].astype(F32)), 0.0)
    for n, xx in enumerate((xl, 1 - xl)):
        piece_wait(xx, same(y_far))
        b2_sends[11 + 5 * n].start()
    for n in range(16):
        load_wo(n).wait()

    def project(xx):
        for yy in (y, y_down, y_up, y_far):
            piece_wait(xx, other(yy))
        half = rem(xx + xh, 2)
        return dot_rows(at[half].reshape(256, 2048), wob[half])

    pre[0:256, 0:WIDE] = project(xl)
    relay(2)
    pre[0:256, 0:WIDE] += project(1 - xl)

    mod = narrow(mods[0])
    modt = narrow(mods[1])
    proj = pre[0:ROWS, 0:WIDE].astype(BF16).astype(F32)
    proj_d = pre[ROWS : 2 * ROWS, 0:WIDE].astype(BF16).astype(F32)
    resid = ys[0] + mod[0:1] * proj
    resid_d = ys[1] + modt[0:1] * proj + mod[0:1] * proj_d
    ys[0] = resid
    ys[1] = resid_d
    mean_i = jnp.mean(resid, axis=-1, keepdims=True)
    dmean_i = jnp.mean(resid_d, axis=-1, keepdims=True)
    cen = resid - mean_i
    square = jnp.sum(cen * cen, axis=-1, keepdims=True)
    cross = jnp.sum(cen * (resid_d - dmean_i), axis=-1, keepdims=True)
    lane = lax.broadcasted_iota(jnp.int32, (ROWS, ROWS), 1)
    packed = jnp.where(
        lane == 0, mean_i, jnp.where(lane == 1, dmean_i, jnp.where(lane == 2, square, cross))
    )
    st[8] = packed.T[0:8, :]
    stat_sib = remote(st.at[8], st.at[9], sts.at[0], str_.at[8], sib)
    stat_sib.start()
    stat_sib.wait_recv()
    st[j] = jnp.concatenate([st[8, 0:4, :], st[9, 0:4, :]], axis=0)

    def stat(k):
        return remote(st.at[j], st.at[j], sts.at[k], str_.at[j], mate(k))

    def stat_send(k, _):
        stat(k).start()
        return 0

    lax.fori_loop(1, 8, stat_send, 0)

    def stat_wait(k, _):
        jj = rem(j + k, 8)
        remote(st.at[jj], st.at[jj], sts.at[k], str_.at[jj], mate(k)).wait_recv()
        return 0

    lax.fori_loop(1, 8, stat_wait, 0)

    def stats(n):
        return jnp.concatenate([st[0:8, n, :], st[0:8, n + 4, :]], axis=0)

    means, dmeans = stats(0), stats(1)
    mean_row = jnp.mean(means, axis=0, keepdims=True)
    dmean_row = jnp.mean(dmeans, axis=0, keepdims=True)
    off = means - mean_row
    var_row = (jnp.sum(stats(2), axis=0, keepdims=True) + WIDE * jnp.sum(off * off, axis=0, keepdims=True)) / D
    cov_row = (
        jnp.sum(stats(3), axis=0, keepdims=True)
        + WIDE * jnp.sum(off * (dmeans - dmean_row), axis=0, keepdims=True)
    ) / D
    inv_row = lax.rsqrt(var_row + 1e-06)
    bend_row = inv_row * inv_row * inv_row * cov_row
    line = lax.broadcasted_iota(jnp.int32, (ROWS, ROWS), 0)
    cols = jnp.where(
        line == 0, mean_row, jnp.where(line == 1, dmean_row, jnp.where(line == 2, inv_row, bend_row))
    ).T
    cen = resid - cols[:, 0:1]
    inv = cols[:, 2:3]
    normed = cen * inv
    normed_d = (resid_d - cols[:, 1:2]) * inv - cen * cols[:, 3:4]
    grow = 1.0 + mod[2:3]
    hb[plane, :, 0:WIDE] = (normed * grow + mod[1:2]).astype(BF16)
    hb[plane, :, WIDE:] = (normed_d * grow + normed * modt[2:3] + modt[1:2]).astype(BF16)

    axes = (((x, x_up, x_down, x_far), (y, y_up, y_down, y_far)), ((y, y_up, y_down, y_far), (x, x_up, x_down, x_far)))
    SELF, UP, DOWN, FAR = range(4)

    def at_chip(flow, first_place, second_place):
        a, b = axes[flow][0][first_place], axes[flow][1][second_place]
        return (a, b) if flow == 0 else (b, a)

    block_sends = []

    def block(flow, first_place, second_place, low=0, count=64):
        xx, yy = at_chip(flow, first_place, second_place)
        slot = xx * 4 + yy
        view = hb.at[slot, pl.ds(64 * flow + low, count), :]
        return lambda n, device: remote(view, view, ds.at[flow, n], dr.at[flow, slot], device)

    counts = [0, 0]

    def block_send(flow, made, device):
        copy = made(counts[flow], device)
        counts[flow] += 1
        copy.start()
        block_sends.append(copy)

    def block_wait(flow, first_place, second_place):
        block(flow, first_place, second_place)(0, sib).wait_recv()

    def beside(flow, first_place, second_place):
        return chip(*at_chip(flow, first_place, second_place))

    def spread_second(flow, first_place):
        for way in (UP, DOWN):
            block_send(flow, block(flow, first_place, SELF), beside(flow, SELF, way))

    def pass_second(flow, first_place):
        block_wait(flow, first_place, DOWN)
        block_send(flow, block(flow, first_place, DOWN, 0, 32), beside(flow, SELF, UP))
        block_wait(flow, first_place, UP)
        block_send(flow, block(flow, first_place, UP, 32, 32), beside(flow, SELF, DOWN))

    for flow in (0, 1):
        for way in (UP, DOWN):
            block_send(flow, block(flow, SELF, SELF), beside(flow, way, SELF))
    for flow in (0, 1):
        spread_second(flow, SELF)
    for flow in (0, 1):
        block_wait(flow, DOWN, SELF)
        block_send(flow, block(flow, DOWN, SELF, 0, 32), beside(flow, UP, SELF))
        block_wait(flow, UP, SELF)
        block_send(flow, block(flow, UP, SELF, 32, 32), beside(flow, DOWN, SELF))
    for flow in (0, 1):
        spread_second(flow, DOWN)
        spread_second(flow, UP)
    for flow in (0, 1):
        block_wait(flow, FAR, SELF)
        spread_second(flow, FAR)
    relay(3)
    for first_place in (SELF, DOWN, UP, FAR):
        for flow in (0, 1):
            pass_second(flow, first_place)

    def feed(arr, xx, yy):
        lanes = slice(WIDE * arr, WIDE * arr + WIDE)
        rows = jnp.concatenate([hb[xx * 4 + yy, :, lanes], hb[(xx + 2) * 4 + yy, :, lanes]], axis=0)
        return jnp.dot(rows, wg[xx * 4 + yy, :, 0:HID], preferred_element_type=F32)

    ring_wait(rem(z + 4, 8))
    for arr in (0, 1):
        part = slice(256 * arr, 256 * arr + 256)
        pre[part, :] = feed(arr, 1 - xl, y)
        pre[part, :] += feed(arr, 1 - xl, y_up)
        pre[part, :] += feed(arr, 1 - xl, y_down)
    for first_place in (SELF, DOWN, UP, FAR):
        for flow in (0, 1):
            block_wait(flow, first_place, FAR)

    def half_of(arr, core):
        return pl.ds(pl.multiple_of(256 * arr + 128 * core, 128), ROWS)

    def swap(arr):
        return remote(pre.at[half_of(arr, 1 - c), :], prex.at[arr], px.at[arr], px.at[2 + arr], sib)

    def share(arr, core):
        view = act.at[half_of(arr, core), :]
        return remote(view, view, px.at[4 + arr], px.at[6 + arr], sib)

    def keep_act(arr, values):
        act[half_of(arr, c), :] = jnp.concatenate(
            [jnp.zeros((ROWS, 48), BF16), values.astype(BF16), jnp.zeros((ROWS, 32), BF16)], axis=1
        )
        share(arr, c).start()

    for arr in (0, 1):
        part = slice(256 * arr, 256 * arr + 256)
        pre[part, :] += feed(arr, 1 - xl, y_far)

        def feed_step(yy, _):
            pre[part, :] += feed(arr, xl, yy)
            return 0

        lax.fori_loop(0, 4, feed_step, 0)
        swap(arr).start()
    root = 0.7978845608028654
    cube = 0.044715
    swap(0).wait_recv()
    before = pre[half_of(0, c), :] + prex[0]
    squared = before * before
    bent = jnp.tanh(root * (before + cube * squared * before))
    half = 0.5 * (1.0 + bent)
    keep_act(0, before * half)
    slope = half + 0.5 * before * (1.0 - bent * bent) * (root * (1.0 + 3.0 * cube * squared))
    swap(1).wait_recv()
    keep_act(1, slope * (pre[half_of(1, c), :] + prex[1]))
    share(0, 1 - c).wait_recv()
    share(1, 1 - c).wait_recv()

    def terms(*pair):
        weight = jnp.concatenate([wg[xx * 4 + yy, :, PACK - 512 :] for xx, yy in pair], axis=0)
        wide = dot_rows(act[...], weight).astype(BF16)
        for n, (xx, yy) in enumerate(pair):
            parts = wide[:, WIDE * n : WIDE * n + WIDE]
            for ee in (0, 1):
                both = jnp.concatenate(
                    [parts[128 * ee : 128 * ee + 128], parts[256 + 128 * ee : 384 + 128 * ee]], axis=1
                )
                ps[0, yy, xx + 2 * ee] = both[0:64]
                ps[1, xx + 2 * ee, yy] = both[64:128]

    major = ((y, y_up, y_down, y_far), (x, x_up, x_down, x_far))
    toward = (
        ((chip(x, y_up), chip(x, y_down)), (chip(x_up, y), chip(x_down, y))),
        ((chip(x_up, y), chip(x_down, y)), (chip(x, y_up), chip(x, y_down))),
    )
    sum_sends = []

    def sum_send(flow, n, src, dst, phase, way):
        copy = remote(src, dst, es.at[flow, n], er.at[flow, n], toward[flow][phase][way])
        copy.start()
        sum_sends.append(copy)

    def sum_wait(flow, n, dst):
        remote(dst, dst, es.at[flow, n], er.at[flow, n], sib).wait_recv()

    def far_out(flow):
        for way in (0, 1):
            src = ps.at[flow, major[flow][FAR], :, pl.ds(32 * way, 32), :]
            sum_send(flow, way, src, ra.at[flow, way], 0, way)

    def plain_out(flow, way):
        place_ = major[flow][(UP, DOWN)[way]]
        rows = pl.ds(32 * (1 - way), 32)
        sum_send(flow, 2 + way, ps.at[flow, place_, :, rows, :], rb.at[flow, way, :, rows, :], 0, way)

    def near_out(flow):
        for way in (0, 1):
            sum_wait(flow, way, ra.at[flow, way])
            place_ = major[flow][(UP, DOWN)[way]]
            rows = pl.ds(32 * way, 32)
            ps[flow, place_, :, rows, :] = (
                ps[flow, place_, :, rows, :].astype(F32) + ra[flow, way].astype(F32)
            ).astype(BF16)
            sum_send(flow, 4 + way, ps.at[flow, place_, :, rows, :], rb.at[flow, way, :, rows, :], 0, way)

    def gathered(flow, place_):
        return (
            ps[flow, major[flow][SELF], place_].astype(F32)
            + rb[flow, 0, place_].astype(F32)
            + rb[flow, 1, place_].astype(F32)
        )

    terms((1 - xl, y_far), (xl, y_far))
    far_out(0)
    terms((xl, y), (xl, y_up))
    terms((xl, y_down), (1 - xl, y_up))
    far_out(1)
    plain_out(0, 0)
    terms((1 - xl, y_down), (1 - xl, y))
    plain_out(0, 1)
    plain_out(1, 0)
    plain_out(1, 1)
    near_out(0)
    near_out(1)
    for flow in (0, 1):
        for way in (0, 1):
            lower, upper = rb.at[flow, way, :, 0:32, :], rb.at[flow, way, :, 32:64, :]
            sum_wait(flow, 2 + way, (upper, lower)[way])
            sum_wait(flow, 4 + way, (lower, upper)[way])
        ta[flow, FAR] = gathered(flow, major[1 - flow][FAR]).astype(BF16)
        for way in (0, 1):
            src = ta.at[flow, FAR, pl.ds(32 * way, 32), :]
            sum_send(flow, 6 + way, src, rc.at[flow, way], 1, way)
        for way in (0, 1):
            ta[flow, (UP, DOWN)[way]] = gathered(flow, major[1 - flow][(UP, DOWN)[way]]).astype(BF16)
            rows = pl.ds(32 * (1 - way), 32)
            src = ta.at[flow, (UP, DOWN)[way], rows, :]
            sum_send(flow, 8 + way, src, rd.at[flow, way, rows, :], 1, way)
    mine_sum = [gathered(flow, major[1 - flow][SELF]) for flow in (0, 1)]
    for flow in (0, 1):
        for way in (0, 1):
            place_ = (UP, DOWN)[way]
            rows = pl.ds(32 * way, 32)
            sum_wait(flow, 6 + way, rc.at[flow, way])
            ta[flow, place_, rows, :] = (ta[flow, place_, rows, :].astype(F32) + rc[flow, way].astype(F32)).astype(BF16)
            sum_send(flow, 10 + way, ta.at[flow, place_, rows, :], rd.at[flow, way, rows, :], 1, way)
    done = []
    for flow in (0, 1):
        rows = pl.ds(64 * flow, 64)
        whole = mine_sum[flow]
        for way in (0, 1):
            lower, upper = rd.at[flow, way, 0:32, :], rd.at[flow, way, 32:64, :]
            sum_wait(flow, 8 + way, (upper, lower)[way])
            sum_wait(flow, 10 + way, (lower, upper)[way])
            whole = whole + rd[flow, way].astype(F32)
        ffn, ffn_d = whole[:, 0:WIDE], whole[:, WIDE:]
        done.append((ys[0, rows, :] + mod[3:4] * ffn, ys[1, rows, :] + modt[3:4] * ffn + mod[3:4] * ffn_d))
    out_ref[...] = jnp.concatenate([done[0][0], done[1][0]], axis=0).T.astype(BF16)
    outt_ref[...] = jnp.concatenate([done[0][1], done[1][1]], axis=0).T.astype(BF16)

    def drain(k, _):
        for pair in (KEY, QUERY, VALUE):
            a1(pair, k - 1).wait_send()
        b1(k - 1).wait_send()
        return 0

    def drain_stat(k, _):
        stat(k).wait_send()
        return 0

    lax.fori_loop(1, 16, drain, 0)
    lax.fori_loop(1, 8, drain_stat, 0)
    stat_sib.wait_send()
    for copy in kv_sends + b2_sends + block_sends + sum_sends + ring_sends + [to_ring]:
        copy.wait_send()
    for arr in (0, 1):
        swap(arr).wait_send()
        share(arr, c).wait_send()


def local(
    hidden_in, hidden_tan, query_in, key_in, value_in, query_tan, key_tan, value_tan,
    output_weight, feed_in, feed_out, modulation, modulation_tan, valid_rows, first_frame,
):
    vmem = pl.BlockSpec(memory_space=pltpu.VMEM)
    hbm = pl.BlockSpec(memory_space=pl.ANY)
    dma = pltpu.SemaphoreType.DMA
    shape = jax.ShapeDtypeStruct((WIDE, ROWS), BF16)
    out, out_d = pl.pallas_call(
        kernel,
        out_shape=(shape, shape),
        in_specs=[pl.BlockSpec(memory_space=pltpu.SMEM)] + [hbm] * 14,
        out_specs=(vmem, vmem),
        scratch_shapes=[
            pltpu.VMEM((6, SUB, 4096), BF16),
            pltpu.VMEM((6, 2048, HD), BF16),
            pltpu.VMEM((256, 2048), F32),
            pltpu.VMEM((256, 2048), F32),
            pltpu.VMEM((256, 2048), BF16),
            pltpu.VMEM((256, 2048), BF16),
            pltpu.VMEM((2, 256, HD), BF16),
            pltpu.VMEM((2, 2, ROWS, 2048), BF16),
            pltpu.VMEM((2, ROWS, 384), BF16),
            pltpu.VMEM((2, WIDE, 2048), BF16),
            pltpu.VMEM((2, WIDE, HID), BF16),
            pltpu.VMEM((WIDE, PACK), BF16),
            pltpu.VMEM((8, WIDE, PACK), BF16),
            pltpu.VMEM((2, ROWS, WIDE), F32),
            pltpu.VMEM((10, 8, ROWS), F32),
            pltpu.VMEM((16, ROWS, 2 * WIDE), BF16),
            pltpu.VMEM((4 * ROWS, HID), F32),
            pltpu.VMEM((2, ROWS, HID), F32),
            pltpu.VMEM((4 * ROWS, 512), BF16),
            pltpu.VMEM((2, 4, 4, 64, 2 * WIDE), BF16),
            pltpu.VMEM((2, 2, 4, 32, 2 * WIDE), BF16),
            pltpu.VMEM((2, 2, 4, 64, 2 * WIDE), BF16),
            pltpu.VMEM((2, 4, 64, 2 * WIDE), BF16),
            pltpu.VMEM((2, 2, 32, 2 * WIDE), BF16),
            pltpu.VMEM((2, 2, 64, 2 * WIDE), BF16),
            pltpu.VMEM((16, ROWS), jnp.int32),
            pltpu.VMEM((2, 4, 384), F32),
            dma((14,)),
            dma((18,)),
            dma((3, 16)),
            dma((3, 16)),
            dma((2, 8)),
            dma((2, 8)),
            dma((8,)),
            dma((4, 2)),
            dma((16,)),
            dma((16,)),
            dma((17,)),
            dma((16,)),
            dma((16,)),
            dma((16,)),
            dma((2, 20)),
            dma((2, 16)),
            dma((8,)),
            dma((2, 12)),
            dma((2, 12)),
        ],
        compiler_params=pltpu.CompilerParams(
            collective_id=0, has_side_effects=True, vmem_limit_bytes=56 * 1024 * 1024
        ),
        cost_estimate=pl.CostEstimate(flops=4_000_000_000, bytes_accessed=20_000_000, transcendentals=1_000_000),
    )(
        first_frame, valid_rows.reshape(16, ROWS), modulation, modulation_tan,
        hidden_in, hidden_tan, query_in, key_in, value_in, query_tan, key_tan, value_tan,
        output_weight.T, feed_in, feed_out.T,
    )
    return out.T, out_d.T


def solution(mesh):
    rows = P("seq", None)
    placed = (rows,) * 8 + (P(None, "tp"), P("seq", "tp"), P("tp", "seq"), P(), P(), P(), P())
    return jax.shard_map(
        local, mesh=mesh, in_specs=placed, out_specs=(P("seq", "tp"), P("seq", "tp")), check_vma=False
    )
```
